128 devices in a mesh: dp: 8 (over y, core), expert: 16 (over z, x).
Axes of the slice: x: 4, y: 4, z: 4, core: 2. Of those that a mesh axis runs over, the one named last changes fastest.
Arguments:
- patches: bfloat16 [65536, 768], P(('dp', 'expert')), may hold values from -6 to 6
- owner_slot: int32 [512], P(('dp', 'expert')), may hold values from 0 to 511, as said below
- segment_ids: int32 [65536], P(('dp', 'expert')), may hold values from 0 to 511, as said below
- block_mask: int32 [512, 4], P(('dp', 'expert')), may hold values from 0 to 1, as said below
- project_in: bfloat16 [768, 2304], replicated, may hold values from -30 to 30
- project_out: bfloat16 [768, 768], replicated, may hold values from -0.21875 to 0.21875
- slot_keys: bfloat16 [768, 128], replicated, may hold values from -30 to 30
- expert_in: bfloat16 [128, 768, 3072], P(('dp', 'expert')), may hold values from -0.21875 to 0.21875
- expert_out: bfloat16 [128, 3072, 768], P(('dp', 'expert')), may hold values from -0.109375 to 0.109375
Outputs:
- layer_out: bfloat16 [65536, 768], P(('dp', 'expert'))
The draws below stay inside these ranges and needn't reach their ends.
Inputs may be any that keep to these rules, and one draw needn't show every extreme that they name: A permutation of the 512 blocks. Devices are numbered over dp then expert, and block g is read by device g // 4; it goes to device owner_slot[g] // 4, which has the same index along expert. Each reading device sends exactly 1 block to each of 4 distinct devices along dp, and each device receives exactly 4 blocks. `segment_ids`: Non-decreasing; the rows of run o (rows o * 512 to o * 512 + 511) carry the image numbers o * 4 to o * 4 + 3, each on one row or more. block_mask[o * 4 + a, b] is 1 when blocks a and b of run o hold rows of a common image, else 0.
All inputs are finite; a program needn't handle non-finite values.
Results may differ from the reference program's by a relative error of at most 0.0095.
The reference program's roundings to bfloat16 on the way count: a program that leaves them out, or rounds other values in their place, can miss the bound.
Values may be sent and summed in bfloat16 or wider, within the bound.
A program may use at most 128 MiB of HBM per device.

```python
import jax
import jax.numpy as jnp
from jax import lax

D = 768
HID = 3072
HEADS = 12
HEAD = 64
BLOCK = 128
BLK_DEV = 4
EXPERTS = 128
TOK_DEV = 512
IMG_DEV = 4
IMAGES = 512
NBLK = 512
TOKENS = 65536
N_DP = 8
N_EXPERT = 16
DEVICES = 128


def permute_each(key, count, length):
    subkeys = jax.random.split(key, count)

    def permute_one(subkey):
        return jax.random.permutation(subkey, length).astype(jnp.int32)
    return jax.vmap(permute_one)(subkeys)


def draw_owner_slot(key, part):
    group = min(N_DP, BLK_DEV)
    shifts = permute_each(jax.random.fold_in(key, 11), N_EXPERT, N_DP)
    orders = permute_each(jax.random.fold_in(key, 12), DEVICES, BLK_DEV)
    reader = jnp.arange(DEVICES, dtype=jnp.int32)
    reader_data = reader // N_EXPERT
    reader_column = reader % N_EXPERT
    chosen = jnp.take_along_axis(shifts[reader_column], orders % group, axis=1)
    owner_data = (reader_data[:, None] + chosen) % N_DP
    owner_device = owner_data * N_EXPERT + reader_column[:, None]
    return (owner_device * BLK_DEV + orders).reshape(-1).astype(jnp.int32)


def image_layout(key):
    tok_dev = BLK_DEV * BLOCK
    subkeys = jax.random.split(jax.random.fold_in(key, 21), DEVICES)

    def one_owner(subkey):
        cuts = jax.random.permutation(subkey, tok_dev - 1)[:BLK_DEV - 1].astype(jnp.int32) + 1
        cuts = jnp.sort(cuts)
        position = jnp.arange(tok_dev, dtype=jnp.int32)
        return jnp.sum((position[:, None] >= cuts[None, :]).astype(jnp.int32), axis=1)
    return jax.vmap(one_owner)(subkeys)


def draw_segment_ids(key, part):
    local = image_layout(key)
    owner = jnp.arange(DEVICES, dtype=jnp.int32)[:, None]
    return (local + owner * BLK_DEV).reshape(-1).astype(jnp.int32)


def draw_block_mask(key, part):
    local = image_layout(key).reshape(DEVICES, BLK_DEV, BLOCK)
    first = local[:, :, 0]
    last = local[:, :, BLOCK - 1]
    lower = jnp.maximum(first[:, :, None], first[:, None, :])
    upper = jnp.minimum(last[:, :, None], last[:, None, :])
    return (lower <= upper).astype(jnp.int32).reshape(DEVICES * BLK_DEV, BLK_DEV)


def draw_project_in(key, part):
    base = jax.random.normal(jax.random.fold_in(key, 31), (D, 3 * D), jnp.float32) * D ** (-0.5)
    return jnp.clip(base, -30.0, 30.0).astype(jnp.bfloat16)


def draw_slot_keys(key, part):
    base = jax.random.normal(jax.random.fold_in(key, 41), (D, EXPERTS), jnp.float32) * D ** (-0.5)
    return jnp.clip(base, -30.0, 30.0).astype(jnp.bfloat16)


def block_levels(own_key, shape, cuts, low, top_value):
    factor_of, own = 1.0, jax.random.fold_in(own_key, 6)
    for dim, blocks in cuts:
        steps = jnp.exp(jax.random.uniform(jax.random.fold_in(own, dim), (blocks,), jnp.float32, low / len(cuts), top_value / len(cuts)))
        factor_of = factor_of * jnp.repeat(steps, shape[dim] // blocks).reshape([-1 if axis == dim else 1 for axis in range(len(shape))])
    return factor_of


def scatter_about(rng, shape, spread, most, pieces=(), kind=jnp.bfloat16):
    array = spread * jax.random.normal(rng, shape, jnp.float32)
    if pieces:
        array = array * block_levels(rng, shape, pieces, -0.22, 0.18)
    return jnp.clip(array, -most, most).astype(kind)


def setup_inputs(seed: int = 0) -> dict:
    arg_keys = jax.random.split(jax.random.key(seed), 10)
    return {
        "patches": scatter_about(arg_keys[0], (TOKENS, D), 1.0, 6.0, ((0, 128),)),
        "owner_slot": draw_owner_slot(jax.random.fold_in(arg_keys[9], 71), 0),
        "segment_ids": draw_segment_ids(jax.random.fold_in(arg_keys[9], 71), 0),
        "block_mask": draw_block_mask(jax.random.fold_in(arg_keys[9], 71), 0),
        "project_in": draw_project_in(jax.random.fold_in(arg_keys[9], 71), 0),
        "project_out": scatter_about(arg_keys[5], (D, D), D ** -0.5, 0.21875),
        "slot_keys": draw_slot_keys(jax.random.fold_in(arg_keys[9], 71), 0),
        "expert_in": scatter_about(arg_keys[7], (EXPERTS, D, HID), D ** -0.5, 0.21875, ((0, 128),)),
        "expert_out": scatter_about(arg_keys[8], (EXPERTS, HID, D), HID ** -0.5, 0.109375, ((0, 128),)),
    }


EPS = 1e-06
NEGATIVE = -1e+30

def layer_norm(values):
    values = values.astype(jnp.float32)
    centred = values - lax.optimization_barrier(jnp.mean(values, axis=-1, keepdims=True))
    variance = lax.optimization_barrier(jnp.mean(centred * centred, axis=-1, keepdims=True))
    return centred * lax.rsqrt(variance + EPS)

def rounded(values):
    return lax.optimization_barrier(values.astype(jnp.bfloat16)).astype(jnp.float32)

def reference(patches, owner_slot, segment_ids, block_mask, project_in, project_out, slot_keys, expert_in, expert_out):
    width = patches.shape[1]
    highest = lax.Precision.HIGHEST
    blocks = patches.reshape(NBLK, BLOCK, width)
    ordered_blocks = jnp.zeros_like(blocks).at[owner_slot].set(blocks)
    ordered_all = ordered_blocks.reshape(DEVICES, TOK_DEV, width)
    seg_all = segment_ids.reshape(DEVICES, TOK_DEV)
    mask_all = block_mask.reshape(DEVICES, BLK_DEV, BLK_DEV)
    block_of = jnp.arange(TOK_DEV, dtype=jnp.int32) // BLOCK
    image_range = jnp.arange(IMG_DEV, dtype=jnp.int32)

    def front(inputs):
        ordered, seg_row, mask_row = inputs
        normed = layer_norm(ordered).astype(jnp.bfloat16)
        joint = rounded(jnp.dot(normed, project_in, preferred_element_type=jnp.float32))
        queries = joint[:, :width].reshape(TOK_DEV, HEADS, HEAD)
        key_rows = joint[:, width:2 * width].reshape(TOK_DEV, HEADS, HEAD)
        value_rows = joint[:, 2 * width:].reshape(TOK_DEV, HEADS, HEAD)
        linked = (seg_row[:, None] == seg_row[None, :]) & (mask_row[block_of][:, block_of] == 1)
        scores = jnp.einsum('qhd,khd->hqk', queries, key_rows, precision=highest) * HEAD ** (-0.5)
        scores = jnp.where(linked[None], scores, NEGATIVE)
        raised = jnp.exp(scores - lax.optimization_barrier(jnp.max(scores, axis=2, keepdims=True)))
        weights = rounded(raised / lax.optimization_barrier(jnp.sum(raised, axis=2, keepdims=True)))
        context = jnp.einsum('hqk,khd->qhd', weights, value_rows, precision=highest).reshape(TOK_DEV, width).astype(jnp.bfloat16)
        hidden = (ordered.astype(jnp.float32) + jnp.dot(context, project_out, preferred_element_type=jnp.float32)).astype(jnp.bfloat16)
        moe_normed = lax.optimization_barrier(layer_norm(hidden).astype(jnp.bfloat16))
        logits = jnp.dot(moe_normed, slot_keys, preferred_element_type=jnp.float32)
        local_image = seg_row % IMG_DEV
        member = local_image[None, :] == image_range[:, None]
        member_float = member.astype(jnp.float32)
        column_max = lax.optimization_barrier(jnp.max(jnp.where(member[:, :, None], logits[None], NEGATIVE), axis=1))
        raised_slots = jnp.exp(logits - column_max[local_image])
        totals = jnp.dot(member_float, raised_slots, precision=highest)
        dispatch = rounded(raised_slots / totals[local_image])
        slot_in = jnp.einsum('st,te,td->sed', member_float, dispatch, moe_normed.astype(jnp.float32), precision=highest).astype(jnp.bfloat16)
        slot_raised = jnp.exp(logits - lax.optimization_barrier(jnp.max(logits, axis=1, keepdims=True)))
        combine = (slot_raised / lax.optimization_barrier(jnp.sum(slot_raised, axis=1, keepdims=True))).astype(jnp.bfloat16)
        return (hidden, slot_in, combine, local_image)
    hidden_all, slot_all, combine_all, local_all = lax.map(front, (ordered_all, seg_all, mask_all))
    slots = jnp.swapaxes(slot_all.reshape(IMAGES, EXPERTS, width), 0, 1)

    def expert_step(inputs):
        slot_column, weight_in, weight_out = inputs
        inner = jnp.dot(slot_column, weight_in, preferred_element_type=jnp.float32)
        inner = jax.nn.gelu(inner, approximate=False).astype(jnp.bfloat16)
        return jnp.dot(inner, weight_out, preferred_element_type=jnp.float32).astype(jnp.bfloat16)
    produced = lax.map(expert_step, (slots, expert_in, expert_out))
    slot_out_all = jnp.swapaxes(produced, 0, 1).reshape(DEVICES, IMG_DEV, EXPERTS, width)

    def back(inputs):
        hidden, combine, local_image, slot_out = inputs
        member_float = (local_image[None, :] == image_range[:, None]).astype(jnp.float32)
        combine_float = lax.optimization_barrier(combine).astype(jnp.float32)
        mixture = jnp.einsum('st,te,sed->td', member_float, combine_float, slot_out.astype(jnp.float32), precision=highest)
        hidden_float = lax.optimization_barrier(hidden).astype(jnp.float32)
        return (hidden_float + mixture).astype(jnp.bfloat16)
    result = lax.map(back, (hidden_all, combine_all, local_all, slot_out_all))
    return result.reshape(TOKENS, width)
```

```python
import jax
import jax.numpy as jnp
from jax import lax
from jax.experimental import pallas as pl
from jax.experimental.pallas import tpu as pltpu
from jax.sharding import PartitionSpec as P

HEADS = 12
HEAD = 64
WIDTH = 768
HALF = WIDTH // 2
HIDDEN = 3072
ROWS = 512
BLOCK = 128
BLOCKS = 4
DP = 8
PEERS = 128
EPS = 1e-06
NEGATIVE = -1e30
GROUPS = 2
GROUP_PEERS = PEERS // GROUPS
CHUNK = 32
MESH = pl.DeviceIdType.MESH
F32 = jnp.float32
BF16 = jnp.bfloat16


def matmul(left, right):
    return jnp.dot(left, right, preferred_element_type=F32)


def matmul_nt(left, right):
    return lax.dot_general(
        left, right, (((1,), (1,)), ((), ())), preferred_element_type=F32
    )


def layer_norm(values):
    centred = values - jnp.mean(values, axis=-1, keepdims=True)
    variance = jnp.mean(centred * centred, axis=-1, keepdims=True)
    return centred * lax.rsqrt(variance + EPS)


def gelu(values):
    return 0.5 * values * (1.0 + lax.erf(values * 0.7071067811865476))


def iota(shape, dim):
    return lax.broadcasted_iota(jnp.int32, shape, dim)


def one_hot(condition):
    return jnp.where(condition, 1.0, 0.0).astype(BF16)


def kernel(
    patches_hbm, owner_ref, segment_ref, mask_ref, in_hbm, out_hbm, keys_hbm, up_hbm, down_hbm,
    result_ref,
    patches, w_in, w_out, w_keys, w_up, w_down,
    stage, slots, place_out, place_in,
    seg_col, image_col, bias, ordered, normed, joint, values_ones, context, hidden, moe_normed,
    slot_send, slot_recv, back_send, back_recv, rows_in, rows_out, mix_weights,
    load_sem, block_send_sem, block_recv_sem, place_send_sem, place_recv_sem,
    slot_send_sem, slot_recv_sem, back_send_sem, back_recv_sem,
):
    dp, ex = lax.axis_index("dp"), lax.axis_index("expert")
    y, core = lax.div(dp, 2), lax.rem(dp, 2)
    z, x = lax.div(ex, 4), lax.rem(ex, 4)

    def ahead(k):
        ax = lax.rem(k, 4)
        az = lax.rem(lax.div(k, 4) + ax, 4)
        ay = lax.rem(lax.div(k, 16) + ax, 4)
        return ax, ay, az, lax.div(k, 64)

    def peer(k, sign):
        ax, ay, az, ac = ahead(k)
        to_y, to_c = lax.rem(y + sign * ay + 4, 4), lax.rem(core + ac, 2)
        to_z, to_x = lax.rem(z + sign * az + 4, 4), lax.rem(x + sign * ax + 4, 4)
        return (to_y * 2 + to_c, to_z * 4 + to_x)

    barrier = pltpu.get_barrier_semaphore()

    def greet(k, carry):
        pl.semaphore_signal(barrier, inc=1, device_id=peer(k, 1), device_id_type=MESH)
        return carry

    lax.fori_loop(1, PEERS, greet, 0)

    loads = [
        pltpu.make_async_copy(source, target, load_sem.at[i])
        for i, (source, target) in enumerate(
            (
                (patches_hbm, patches),
                (in_hbm, w_in),
                (keys_hbm, w_keys),
                (out_hbm, w_out),
                (up_hbm.at[0], w_up),
                (down_hbm.at[0], w_down),
            )
        )
    ]
    for load in loads:
        load.start()

    targets = [lax.div(owner_ref[b], BLOCKS * PEERS // DP) for b in range(BLOCKS)]
    places = [lax.rem(owner_ref[b], BLOCKS) for b in range(BLOCKS)]

    def dp_peer(a, sign):
        return lax.rem(y + sign * (a % 4) + 4, 4) * 2 + lax.rem(core + a // 4, 2)

    loads[0].wait()
    for a in range(DP):
        to = dp_peer(a, 1)
        index, place = jnp.int32(0), jnp.int32(-1)
        for b in range(BLOCKS):
            hit = targets[b] == to
            index = jnp.where(hit, b, index)
            place = jnp.where(hit, places[b], place)
        if a:
            stage[a] = patches[index]
            place_out[a] = jnp.full((8, 128), place, jnp.int32)
        else:
            slots[0] = patches[index]
            place_in[0] = jnp.full((8, 128), place, jnp.int32)

    pl.semaphore_wait(barrier, PEERS - 1)
    sends = []
    for a in (2, 6, 1, 3, 5, 7, 4):
        to = (dp_peer(a, 1), ex)
        for source, target, send, recv in (
            (place_out, place_in, place_send_sem, place_recv_sem),
            (stage, slots, block_send_sem, block_recv_sem),
        ):
            copy = pltpu.make_async_remote_copy(
                src_ref=source.at[a], dst_ref=target.at[a], send_sem=send.at[a], recv_sem=recv.at[a],
                device_id=to, device_id_type=MESH,
            )
            copy.start()
            sends.append(copy)

    segment = segment_ref[...]
    seg_col[...] = jnp.transpose(jnp.broadcast_to(segment.astype(F32), (BLOCK, ROWS)))
    image_col[...] = jnp.transpose(
        jnp.broadcast_to((segment & (BLOCKS - 1)).astype(F32), (BLOCK, ROWS))
    )
    for a in range(BLOCKS):
        for b in range(BLOCKS):
            link = jnp.where(mask_ref[a, b] == 1, 0.0, NEGATIVE)
            rows, columns = slice(a * BLOCK, (a + 1) * BLOCK), slice(b * BLOCK, (b + 1) * BLOCK)
            same = seg_col[rows, :] == segment[:, columns].astype(F32)
            bias[rows, columns] = jnp.where(same, link, NEGATIVE)
    values_ones[:, BLOCK:] = jnp.ones((ROWS, BLOCK), BF16)

    k_lane = iota((PEERS, PEERS), 1)
    ax = k_lane & 3
    az = ((k_lane >> 2) + ax) & 3
    ay = ((k_lane >> 4) + ax) & 3
    ac = k_lane >> 6
    expert_at = ((((y + ay) & 3) * 2 + ((core + ac) & 1)) * 4 + ((z + az) & 3)) * 4 + ((x + ax) & 3)
    reorder = one_hot(iota((PEERS, PEERS), 0) == expert_at)
    for load in loads[1:3]:
        load.wait()
    keys = matmul(w_keys[...], reorder).astype(BF16)

    for copy in sends:
        copy.wait()
    for p in range(BLOCKS):
        where_from = jnp.zeros((8, 128), jnp.int32)
        for a in range(1, DP):
            where_from = jnp.where(place_in[a] == p, a, where_from)
        index = jnp.max(where_from)
        block = slots[index]
        rows = slice(p * BLOCK, (p + 1) * BLOCK)
        ordered[rows, :] = block
        normed[rows, :] = layer_norm(block.astype(F32)).astype(BF16)
    joint[...] = matmul(normed[...], w_in[...]).astype(BF16)

    lane = iota((BLOCK, BLOCK), 1)
    first = lane < HEAD

    def head_pair(i, carry):
        columns = pl.ds(pl.multiple_of(i * BLOCK, BLOCK), BLOCK)
        key_rows = joint[:, pl.ds(pl.multiple_of(WIDTH + i * BLOCK, BLOCK), BLOCK)]
        values_ones[:, :BLOCK] = joint[:, pl.ds(pl.multiple_of(2 * WIDTH + i * BLOCK, BLOCK), BLOCK)]
        both = values_ones[...]
        for q in range(BLOCKS):
            rows = slice(q * BLOCK, (q + 1) * BLOCK)
            queries = joint[rows, columns]
            parts = []
            for h in range(2):
                scale = jnp.where(first == (h == 0), HEAD**-0.5, 0.0).astype(BF16)
                scores = matmul_nt(queries * scale, key_rows) + bias[rows, :]
                raised = jnp.exp(scores - jnp.max(scores, axis=1, keepdims=True))
                sums = matmul(raised.astype(BF16), both)
                parts.append(sums[:, :BLOCK] / sums[:, BLOCK:])
            context[rows, columns] = jnp.where(first, parts[0], parts[1]).astype(BF16)
        return carry

    lax.fori_loop(0, HEADS // 2, head_pair, 0)

    loads[3].wait()
    added = ordered[...].astype(F32) + matmul(context[...], w_out[...])
    hidden[...] = added.astype(BF16)
    moe_normed[...] = layer_norm(hidden[...].astype(F32)).astype(BF16)
    logits = matmul(moe_normed[...], keys)

    image = image_col[...]
    members = [image == float(s) for s in range(BLOCKS)]

    def by_image(per_image):
        chosen = per_image[0]
        for s in range(1, BLOCKS):
            chosen = jnp.where(members[s], per_image[s], chosen)
        return chosen

    column_max = [
        jnp.max(jnp.where(m, logits, NEGATIVE), axis=0, keepdims=True) for m in members
    ]
    raised = jnp.exp(logits - by_image(column_max))
    totals = [jnp.sum(jnp.where(m, raised, 0.0), axis=0, keepdims=True) for m in members]
    dispatch = jnp.transpose(raised / by_image(totals)).astype(BF16)

    halves = jnp.concatenate([moe_normed[:, :HALF], moe_normed[:, HALF:]], axis=0)
    image_row = segment & (BLOCKS - 1)
    eight = CHUNK * 8
    row = iota((eight, ROWS), 0)
    spread = one_hot(lax.broadcasted_iota(jnp.int32, (eight, CHUNK), 0) >> 3 == iota((eight, CHUNK), 1))
    own_image = ((row >> 1) & 3) == image_row

    def send_slots(k, carry):
        group = lax.div(k, GROUP_PEERS)
        pltpu.make_async_remote_copy(
            src_ref=slot_send.at[k], dst_ref=slot_recv.at[k],
            send_sem=slot_send_sem, recv_sem=slot_recv_sem.at[group],
            device_id=peer(k, 1), device_id_type=MESH,
        ).start()
        return carry

    for c in range(PEERS // CHUNK):
        wide = matmul(spread, dispatch[c * CHUNK : (c + 1) * CHUNK, :])
        weights = [
            jnp.where(own_image & ((row & 1) == h), wide, 0.0).astype(BF16) for h in range(2)
        ]
        summed = matmul(jnp.concatenate(weights, axis=1), halves)
        slot_send[c * CHUNK : (c + 1) * CHUNK] = summed.reshape(CHUNK, 8, HALF).astype(BF16)
        if c == 0:
            pltpu.make_async_copy(slot_send.at[0], slot_recv.at[0], slot_recv_sem.at[0]).start()
        lax.fori_loop(max(1, c * CHUNK), (c + 1) * CHUNK, send_slots, 0)

    top = jnp.exp(logits - jnp.max(logits, axis=1, keepdims=True))
    combine = (top / jnp.sum(top, axis=1, keepdims=True)).astype(BF16)
    column = iota((BLOCK, PEERS * 8), 1)
    repeat = one_hot(iota((PEERS, PEERS * 8), 1) >> 3 == iota((PEERS, PEERS * 8), 0))
    for q in range(BLOCKS):
        rows = slice(q * BLOCK, (q + 1) * BLOCK)
        wide = matmul(combine[rows, :], repeat)
        for c in range(PEERS * 8 // BLOCK):
            columns = slice(c * BLOCK, (c + 1) * BLOCK)
            slot = column[:, columns]
            own = ((slot >> 1) & 3).astype(F32) == image[rows, :]
            for h in range(2):
                mix_weights[h, rows, columns] = jnp.where(
                    own & ((slot & 1) == h), wide[:, columns], 0.0
                ).astype(BF16)

    def send_back(k, carry):
        group = lax.div(k, GROUP_PEERS)
        pltpu.make_async_remote_copy(
            src_ref=back_send.at[k], dst_ref=back_recv.at[k],
            send_sem=back_send_sem, recv_sem=back_recv_sem.at[group],
            device_id=peer(k, -1), device_id_type=MESH,
        ).start()
        return carry

    for load in loads[4:]:
        load.wait()
    four = CHUNK * 4
    pick = [one_hot(iota((four, eight), 1) == 2 * iota((four, eight), 0) + h) for h in range(2)]
    weave_q = iota((eight, eight), 1)
    weave = one_hot(
        iota((eight, eight), 0) == 2 * (weave_q & (four - 1)) + lax.shift_right_logical(weave_q, 7)
    )
    for g in range(GROUPS):
        group = slot_recv.at[pl.ds(g * GROUP_PEERS, GROUP_PEERS)]
        pltpu.make_async_copy(group, group, slot_recv_sem.at[g]).wait()
        for c in range(GROUP_PEERS // CHUNK):
            start = g * GROUP_PEERS + c * CHUNK
            arrived = slot_recv[start : start + CHUNK].reshape(eight, HALF)
            for h in range(2):
                rows_in[c * four : (c + 1) * four, h * HALF : (h + 1) * HALF] = matmul(
                    pick[h], arrived
                ).astype(BF16)
        left = rows_in[...]
        total = jnp.zeros((GROUP_PEERS * 4, WIDTH), F32)
        step = 512
        for c in range(HIDDEN // step):
            inner = gelu(matmul(left, w_up[:, c * step : (c + 1) * step])).astype(BF16)
            total = total + matmul(inner, w_down[c * step : (c + 1) * step, :])
        rows_out[...] = total.astype(BF16)
        for c in range(GROUP_PEERS // CHUNK):
            start = g * GROUP_PEERS + c * CHUNK
            rows = slice(c * four, (c + 1) * four)
            stacked = jnp.concatenate([rows_out[rows, :HALF], rows_out[rows, HALF:]], axis=0)
            back_send[start : start + CHUNK] = (
                matmul(weave, stacked).reshape(CHUNK, 8, HALF).astype(BF16)
            )
        if g == 0:
            pltpu.make_async_copy(back_send.at[0], back_recv.at[0], back_recv_sem.at[0]).start()
        lax.fori_loop(max(1, g * GROUP_PEERS), (g + 1) * GROUP_PEERS, send_back, 0)

    mixture = [jnp.zeros((ROWS, HALF), F32)] * 2
    for g in range(GROUPS):
        group = back_recv.at[pl.ds(g * GROUP_PEERS, GROUP_PEERS)]
        pltpu.make_async_copy(group, group, back_recv_sem.at[g]).wait()
        arrived = back_recv[g * GROUP_PEERS : (g + 1) * GROUP_PEERS].reshape(GROUP_PEERS * 8, HALF)
        columns = slice(g * GROUP_PEERS * 8, (g + 1) * GROUP_PEERS * 8)
        mixture = [mixture[h] + matmul(mix_weights[h, :, columns], arrived) for h in range(2)]
    for h in range(2):
        columns = slice(h * HALF, (h + 1) * HALF)
        result_ref[:, columns] = (hidden[:, columns].astype(F32) + mixture[h]).astype(BF16)

    sent = slot_send.at[pl.ds(1, PEERS - 1)]
    pltpu.make_async_copy(sent, sent, slot_send_sem).wait()
    sent = back_send.at[pl.ds(1, PEERS - 1)]
    pltpu.make_async_copy(sent, sent, back_send_sem).wait()


def per_device(
    patches, owner_slot, segment_ids, block_mask, project_in, project_out, slot_keys, expert_in, expert_out
):
    hbm, smem = pl.BlockSpec(memory_space=pl.ANY), pl.BlockSpec(memory_space=pltpu.SMEM)
    vmem = pl.BlockSpec(memory_space=pltpu.VMEM)
    exchange = pltpu.VMEM((PEERS, 8, HALF), BF16)
    dma = pltpu.SemaphoreType.DMA
    return pl.pallas_call(
        kernel,
        out_shape=jax.ShapeDtypeStruct((ROWS, WIDTH), BF16),
        in_specs=[hbm, smem, vmem, smem, hbm, hbm, hbm, hbm, hbm],
        out_specs=vmem,
        scratch_shapes=[
            pltpu.VMEM((BLOCKS, BLOCK, WIDTH), BF16),
            pltpu.VMEM((WIDTH, 3 * WIDTH), BF16),
            pltpu.VMEM((WIDTH, WIDTH), BF16),
            pltpu.VMEM((WIDTH, PEERS), BF16),
            pltpu.VMEM((WIDTH, HIDDEN), BF16),
            pltpu.VMEM((HIDDEN, WIDTH), BF16),
            pltpu.VMEM((DP, BLOCK, WIDTH), BF16),
            pltpu.VMEM((DP, BLOCK, WIDTH), BF16),
            pltpu.VMEM((DP, 8, 128), jnp.int32),
            pltpu.VMEM((DP, 8, 128), jnp.int32),
            pltpu.VMEM((ROWS, BLOCK), F32),
            pltpu.VMEM((ROWS, BLOCK), F32),
            pltpu.VMEM((ROWS, ROWS), F32),
            pltpu.VMEM((ROWS, WIDTH), BF16),
            pltpu.VMEM((ROWS, WIDTH), BF16),
            pltpu.VMEM((ROWS, 3 * WIDTH), BF16),
            pltpu.VMEM((ROWS, 2 * BLOCK), BF16),
            pltpu.VMEM((ROWS, WIDTH), BF16),
            pltpu.VMEM((ROWS, WIDTH), BF16),
            pltpu.VMEM((ROWS, WIDTH), BF16),
            exchange,
            exchange,
            exchange,
            exchange,
            pltpu.VMEM((GROUP_PEERS * 4, WIDTH), BF16),
            pltpu.VMEM((GROUP_PEERS * 4, WIDTH), BF16),
            pltpu.VMEM((2, ROWS, PEERS * 8), BF16),
            dma((6,)),
            dma((DP,)),
            dma((DP,)),
            dma((DP,)),
            dma((DP,)),
            dma,
            dma((GROUPS,)),
            dma,
            dma((GROUPS,)),
        ],
        compiler_params=pltpu.CompilerParams(
            collective_id=0, has_side_effects=True, vmem_limit_bytes=58 * 1024 * 1024
        ),
    )(
        patches.reshape(BLOCKS, BLOCK, WIDTH),
        owner_slot,
        segment_ids.reshape(1, ROWS),
        block_mask,
        project_in,
        project_out,
        slot_keys,
        expert_in,
        expert_out,
    )


def solution(mesh):
    in_specs = (
        P(("dp", "expert"), None),
        P(("dp", "expert")),
        P(("dp", "expert")),
        P(("dp", "expert"), None),
        P(),
        P(),
        P(),
        P(("dp", "expert"), None, None),
        P(("dp", "expert"), None, None),
    )
    return jax.shard_map(
        per_device,
        mesh=mesh,
        in_specs=in_specs,
        out_specs=P(("dp", "expert"), None),
        check_vma=False,
    )
```

```python
import jax
import jax.numpy as jnp
from jax import lax
from jax.experimental import pallas as pl
from jax.experimental.pallas import tpu as pltpu
from jax.sharding import PartitionSpec as P

HEADS = 12
HEAD = 64
WIDTH = 768
HALF = WIDTH // 2
HIDDEN = 3072
ROWS = 512
BLOCK = 128
BLOCKS = 4
DP = 8
PEERS = 128
EPS = 1e-06
NEGATIVE = -1e30
GROUPS = 2
GROUP_PEERS = PEERS // GROUPS
CHUNK = 32
MESH = pl.DeviceIdType.MESH
F32 = jnp.float32
BF16 = jnp.bfloat16


def matmul(left, right):
    return jnp.dot(left, right, preferred_element_type=F32)


def matmul_nt(left, right):
    return lax.dot_general(
        left, right, (((1,), (1,)), ((), ())), preferred_element_type=F32
    )


def layer_norm(values):
    centred = values - jnp.mean(values, axis=-1, keepdims=True)
    variance = jnp.mean(centred * centred, axis=-1, keepdims=True)
    return centred * lax.rsqrt(variance + EPS)


def gelu(values):
    return 0.5 * values * (1.0 + lax.erf(values * 0.7071067811865476))


def iota(shape, dim):
    return lax.broadcasted_iota(jnp.int32, shape, dim)


def one_hot(condition):
    return jnp.where(condition, 1.0, 0.0).astype(BF16)


def kernel(
    patches_hbm, owner_ref, segment_ref, mask_ref, in_hbm, out_hbm, keys_hbm, up_hbm, down_hbm,
    result_ref,
    patches, w_in, w_out, w_keys, w_up, w_down,
    stage, slots, place_out, place_in,
    seg_col, image_col, bias, ordered, normed, joint, values_ones, context, hidden, moe_normed,
    slot_send, slot_recv, back_send, back_recv, rows_in, rows_out, mix_weights,
    load_sem, block_send_sem, block_recv_sem, place_send_sem, place_recv_sem,
    slot_send_sem, slot_recv_sem, back_send_sem, back_recv_sem, plane_sem, cube_sem,
):
    dp, ex = lax.axis_index("dp"), lax.axis_index("expert")
    y, core = lax.div(dp, 2), lax.rem(dp, 2)
    z, x = lax.div(ex, 4), lax.rem(ex, 4)

    dp_at = [[lax.rem(y + ay, 4) * 2 + lax.rem(core + ac, 2) for ac in range(2)] for ay in range(4)]
    ex_at = [[lax.rem(z + az, 4) * 4 + lax.rem(x + ax, 4) for ax in range(4)] for az in range(4)]

    def peer(k, sign):
        ax = k % 4
        ay, az, ac = (k // 16 + ax) % 4, (k // 4 + ax) % 4, k // 64
        return (dp_at[sign * ay % 4][ac], ex_at[sign * az % 4][sign * ax % 4])

    barrier = pltpu.get_barrier_semaphore()
    line_dp = [(dp_at[a % 4][a // 4], ex) for a in range(1, DP)]
    line_z = [(dp, ex_at[a][0]) for a in range(1, 4)]
    line_x = [(dp, ex_at[0][a]) for a in range(1, 4)]

    def tell(semaphore, line):
        for device in line:
            pl.semaphore_signal(semaphore, inc=1, device_id=device, device_id_type=MESH)

    tell(barrier, line_dp + line_z + line_x)

    loads = [
        pltpu.make_async_copy(source, target, load_sem.at[i])
        for i, (source, target) in enumerate(
            (
                (patches_hbm, patches),
                (in_hbm, w_in),
                (keys_hbm, w_keys),
                (out_hbm, w_out),
                (up_hbm.at[0], w_up),
                (down_hbm.at[0], w_down),
            )
        )
    ]
    for load in loads:
        load.start()

    targets = [lax.div(owner_ref[b], BLOCKS * PEERS // DP) for b in range(BLOCKS)]
    places = [lax.rem(owner_ref[b], BLOCKS) for b in range(BLOCKS)]

    loads[0].wait()
    for a in range(DP):
        to = dp_at[a % 4][a // 4]
        index, place = jnp.int32(0), jnp.int32(-1)
        for b in range(BLOCKS):
            hit = targets[b] == to
            index = jnp.where(hit, b, index)
            place = jnp.where(hit, places[b], place)
        if a:
            stage[a] = patches[index]
            place_out[a] = jnp.full((8, 128), place, jnp.int32)
        else:
            slots[0] = patches[index]
            place_in[0] = jnp.full((8, 128), place, jnp.int32)

    pl.semaphore_wait(barrier, 13)
    sends = []
    for a in (2, 6, 1, 3, 5, 7, 4):
        to = (dp_at[a % 4][a // 4], ex)
        for source, target, send, recv in (
            (place_out, place_in, place_send_sem, place_recv_sem),
            (stage, slots, block_send_sem, block_recv_sem),
        ):
            copy = pltpu.make_async_remote_copy(
                src_ref=source.at[a], dst_ref=target.at[a], send_sem=send.at[a], recv_sem=recv.at[a],
                device_id=to, device_id_type=MESH,
            )
            copy.start()
            sends.append(copy)

    tell(plane_sem, line_x)
    segment = segment_ref[...]
    seg_col[...] = jnp.transpose(jnp.broadcast_to(segment.astype(F32), (BLOCK, ROWS)))
    image_col[...] = jnp.transpose(
        jnp.broadcast_to((segment & (BLOCKS - 1)).astype(F32), (BLOCK, ROWS))
    )
    for a in range(BLOCKS):
        for b in range(BLOCKS):
            link = jnp.where(mask_ref[a, b] == 1, 0.0, NEGATIVE)
            rows, columns = slice(a * BLOCK, (a + 1) * BLOCK), slice(b * BLOCK, (b + 1) * BLOCK)
            same = seg_col[rows, :] == segment[:, columns].astype(F32)
            bias[rows, columns] = jnp.where(same, link, NEGATIVE)
    values_ones[:, BLOCK:] = jnp.ones((ROWS, BLOCK), BF16)

    pl.semaphore_wait(plane_sem, 3)
    tell(cube_sem, line_dp)
    k_lane = iota((PEERS, PEERS), 1)
    ax = k_lane & 3
    az = ((k_lane >> 2) + ax) & 3
    ay = ((k_lane >> 4) + ax) & 3
    ac = k_lane >> 6
    expert_at = ((((y + ay) & 3) * 2 + ((core + ac) & 1)) * 4 + ((z + az) & 3)) * 4 + ((x + ax) & 3)
    reorder = one_hot(iota((PEERS, PEERS), 0) == expert_at)
    for load in loads[1:3]:
        load.wait()
    keys = matmul(w_keys[...], reorder).astype(BF16)

    for copy in sends:
        copy.wait()
    pl.semaphore_wait(cube_sem, DP - 1)
    for p in range(BLOCKS):
        where_from = jnp.zeros((8, 128), jnp.int32)
        for a in range(1, DP):
            where_from = jnp.where(place_in[a] == p, a, where_from)
        index = jnp.max(where_from)
        block = slots[index]
        rows = slice(p * BLOCK, (p + 1) * BLOCK)
        ordered[rows, :] = block
        normed[rows, :] = layer_norm(block.astype(F32)).astype(BF16)
    joint[...] = matmul(normed[...], w_in[...]).astype(BF16)

    lane = iota((BLOCK, BLOCK), 1)
    first = lane < HEAD

    def head_pair(i, carry):
        columns = pl.ds(pl.multiple_of(i * BLOCK, BLOCK), BLOCK)
        key_rows = joint[:, pl.ds(pl.multiple_of(WIDTH + i * BLOCK, BLOCK), BLOCK)]
        values_ones[:, :BLOCK] = joint[:, pl.ds(pl.multiple_of(2 * WIDTH + i * BLOCK, BLOCK), BLOCK)]
        both = values_ones[...]
        for q in range(BLOCKS):
            rows = slice(q * BLOCK, (q + 1) * BLOCK)
            queries = joint[rows, columns]
            parts = []
            for h in range(2):
                scale = jnp.where(first == (h == 0), HEAD**-0.5, 0.0).astype(BF16)
                scores = matmul_nt(queries * scale, key_rows) + bias[rows, :]
                raised = jnp.exp(scores - jnp.max(scores, axis=1, keepdims=True))
                sums = matmul(raised.astype(BF16), both)
                parts.append(sums[:, :BLOCK] / sums[:, BLOCK:])
            context[rows, columns] = jnp.where(first, parts[0], parts[1]).astype(BF16)
        return carry

    lax.fori_loop(0, HEADS // 2, head_pair, 0)

    loads[3].wait()
    added = ordered[...].astype(F32) + matmul(context[...], w_out[...])
    hidden[...] = added.astype(BF16)
    moe_normed[...] = layer_norm(hidden[...].astype(F32)).astype(BF16)
    logits = matmul(moe_normed[...], keys)

    image = image_col[...]
    members = [image == float(s) for s in range(BLOCKS)]

    def by_image(per_image):
        chosen = per_image[0]
        for s in range(1, BLOCKS):
            chosen = jnp.where(members[s], per_image[s], chosen)
        return chosen

    column_max = [
        jnp.max(jnp.where(m, logits, NEGATIVE), axis=0, keepdims=True) for m in members
    ]
    raised = jnp.exp(logits - by_image(column_max))
    totals = [jnp.sum(jnp.where(m, raised, 0.0), axis=0, keepdims=True) for m in members]
    dispatch = jnp.transpose(raised / by_image(totals)).astype(BF16)

    halves = jnp.concatenate([moe_normed[:, :HALF], moe_normed[:, HALF:]], axis=0)
    image_row = segment & (BLOCKS - 1)
    eight = CHUNK * 8
    row = iota((eight, ROWS), 0)
    spread = one_hot(lax.broadcasted_iota(jnp.int32, (eight, CHUNK), 0) >> 3 == iota((eight, CHUNK), 1))
    own_image = ((row >> 1) & 3) == image_row

    def send(k, source, target, send_sem, recv_sem, sign):
        recv = recv_sem.at[k // GROUP_PEERS]
        if k:
            pltpu.make_async_remote_copy(
                src_ref=source.at[k], dst_ref=target.at[k], send_sem=send_sem, recv_sem=recv,
                device_id=peer(k, sign), device_id_type=MESH,
            ).start()
        else:
            pltpu.make_async_copy(source.at[0], target.at[0], recv).start()

    for c in range(PEERS // CHUNK):
        wide = matmul(spread, dispatch[c * CHUNK : (c + 1) * CHUNK, :])
        weights = [
            jnp.where(own_image & ((row & 1) == h), wide, 0.0).astype(BF16) for h in range(2)
        ]
        summed = matmul(jnp.concatenate(weights, axis=1), halves)
        slot_send[c * CHUNK : (c + 1) * CHUNK] = summed.reshape(CHUNK, 8, HALF).astype(BF16)
        for k in range(c * CHUNK, (c + 1) * CHUNK):
            send(k, slot_send, slot_recv, slot_send_sem, slot_recv_sem, 1)

    top = jnp.exp(logits - jnp.max(logits, axis=1, keepdims=True))
    combine = (top / jnp.sum(top, axis=1, keepdims=True)).astype(BF16)
    column = iota((BLOCK, PEERS * 8), 1)
    repeat = one_hot(iota((PEERS, PEERS * 8), 1) >> 3 == iota((PEERS, PEERS * 8), 0))
    for q in range(BLOCKS):
        rows = slice(q * BLOCK, (q + 1) * BLOCK)
        wide = matmul(combine[rows, :], repeat)
        for c in range(PEERS * 8 // BLOCK):
            columns = slice(c * BLOCK, (c + 1) * BLOCK)
            slot = column[:, columns]
            own = ((slot >> 1) & 3).astype(F32) == image[rows, :]
            for h in range(2):
                mix_weights[h, rows, columns] = jnp.where(
                    own & ((slot & 1) == h), wide[:, columns], 0.0
                ).astype(BF16)

    for load in loads[4:]:
        load.wait()
    four = CHUNK * 4
    pick = [one_hot(iota((four, eight), 1) == 2 * iota((four, eight), 0) + h) for h in range(2)]
    weave_q = iota((eight, eight), 1)
    weave = one_hot(
        iota((eight, eight), 0) == 2 * (weave_q & (four - 1)) + lax.shift_right_logical(weave_q, 7)
    )
    for g in range(GROUPS):
        group = slot_recv.at[pl.ds(g * GROUP_PEERS, GROUP_PEERS)]
        pltpu.make_async_copy(group, group, slot_recv_sem.at[g]).wait()
        for c in range(GROUP_PEERS // CHUNK):
            start = g * GROUP_PEERS + c * CHUNK
            arrived = slot_recv[start : start + CHUNK].reshape(eight, HALF)
            for h in range(2):
                rows_in[c * four : (c + 1) * four, h * HALF : (h + 1) * HALF] = matmul(
                    pick[h], arrived
                ).astype(BF16)
        left = rows_in[...]
        total = jnp.zeros((GROUP_PEERS * 4, WIDTH), F32)
        step = 512
        for c in range(HIDDEN // step):
            inner = gelu(matmul(left, w_up[:, c * step : (c + 1) * step])).astype(BF16)
            total = total + matmul(inner, w_down[c * step : (c + 1) * step, :])
        rows_out[...] = total.astype(BF16)
        for c in range(GROUP_PEERS // CHUNK):
            start = g * GROUP_PEERS + c * CHUNK
            rows = slice(c * four, (c + 1) * four)
            stacked = jnp.concatenate([rows_out[rows, :HALF], rows_out[rows, HALF:]], axis=0)
            back_send[start : start + CHUNK] = (
                matmul(weave, stacked).reshape(CHUNK, 8, HALF).astype(BF16)
            )
        for k in range(g * GROUP_PEERS, (g + 1) * GROUP_PEERS):
            send(k, back_send, back_recv, back_send_sem, back_recv_sem, -1)

    mixture = [jnp.zeros((ROWS, HALF), F32)] * 2
    for g in range(GROUPS):
        group = back_recv.at[pl.ds(g * GROUP_PEERS, GROUP_PEERS)]
        pltpu.make_async_copy(group, group, back_recv_sem.at[g]).wait()
        arrived = back_recv[g * GROUP_PEERS : (g + 1) * GROUP_PEERS].reshape(GROUP_PEERS * 8, HALF)
        columns = slice(g * GROUP_PEERS * 8, (g + 1) * GROUP_PEERS * 8)
        mixture = [mixture[h] + matmul(mix_weights[h, :, columns], arrived) for h in range(2)]
    for h in range(2):
        columns = slice(h * HALF, (h + 1) * HALF)
        result_ref[:, columns] = (hidden[:, columns].astype(F32) + mixture[h]).astype(BF16)

    sent = slot_send.at[pl.ds(1, PEERS - 1)]
    pltpu.make_async_copy(sent, sent, slot_send_sem).wait()
    sent = back_send.at[pl.ds(1, PEERS - 1)]
    pltpu.make_async_copy(sent, sent, back_send_sem).wait()


def per_device(
    patches, owner_slot, segment_ids, block_mask, project_in, project_out, slot_keys, expert_in, expert_out
):
    hbm, smem = pl.BlockSpec(memory_space=pl.ANY), pl.BlockSpec(memory_space=pltpu.SMEM)
    vmem = pl.BlockSpec(memory_space=pltpu.VMEM)
    exchange = pltpu.VMEM((PEERS, 8, HALF), BF16)
    dma = pltpu.SemaphoreType.DMA
    return pl.pallas_call(
        kernel,
        out_shape=jax.ShapeDtypeStruct((ROWS, WIDTH), BF16),
        in_specs=[hbm, smem, vmem, smem, hbm, hbm, hbm, hbm, hbm],
        out_specs=vmem,
        scratch_shapes=[
            pltpu.VMEM((BLOCKS, BLOCK, WIDTH), BF16),
            pltpu.VMEM((WIDTH, 3 * WIDTH), BF16),
            pltpu.VMEM((WIDTH, WIDTH), BF16),
            pltpu.VMEM((WIDTH, PEERS), BF16),
            pltpu.VMEM((WIDTH, HIDDEN), BF16),
            pltpu.VMEM((HIDDEN, WIDTH), BF16),
            pltpu.VMEM((DP, BLOCK, WIDTH), BF16),
            pltpu.VMEM((DP, BLOCK, WIDTH), BF16),
            pltpu.VMEM((DP, 8, 128), jnp.int32),
            pltpu.VMEM((DP, 8, 128), jnp.int32),
            pltpu.VMEM((ROWS, BLOCK), F32),
            pltpu.VMEM((ROWS, BLOCK), F32),
            pltpu.VMEM((ROWS, ROWS), F32),
            pltpu.VMEM((ROWS, WIDTH), BF16),
            pltpu.VMEM((ROWS, WIDTH), BF16),
            pltpu.VMEM((ROWS, 3 * WIDTH), BF16),
            pltpu.VMEM((ROWS, 2 * BLOCK), BF16),
            pltpu.VMEM((ROWS, WIDTH), BF16),
            pltpu.VMEM((ROWS, WIDTH), BF16),
            pltpu.VMEM((ROWS, WIDTH), BF16),
            exchange,
            exchange,
            exchange,
            exchange,
            pltpu.VMEM((GROUP_PEERS * 4, WIDTH), BF16),
            pltpu.VMEM((GROUP_PEERS * 4, WIDTH), BF16),
            pltpu.VMEM((2, ROWS, PEERS * 8), BF16),
            dma((6,)),
            dma((DP,)),
            dma((DP,)),
            dma((DP,)),
            dma((DP,)),
            dma,
            dma((GROUPS,)),
            dma,
            dma((GROUPS,)),
            pltpu.SemaphoreType.REGULAR,
            pltpu.SemaphoreType.REGULAR,
        ],
        compiler_params=pltpu.CompilerParams(
            collective_id=0, has_side_effects=True, vmem_limit_bytes=58 * 1024 * 1024
        ),
    )(
        patches.reshape(BLOCKS, BLOCK, WIDTH),
        owner_slot,
        segment_ids.reshape(1, ROWS),
        block_mask,
        project_in,
        project_out,
        slot_keys,
        expert_in,
        expert_out,
    )


def solution(mesh):
    in_specs = (
        P(("dp", "expert"), None),
        P(("dp", "expert")),
        P(("dp", "expert")),
        P(("dp", "expert"), None),
        P(),
        P(),
        P(),
        P(("dp", "expert"), None, None),
        P(("dp", "expert"), None, None),
    )
    return jax.shard_map(
        per_device,
        mesh=mesh,
        in_specs=in_specs,
        out_specs=P(("dp", "expert"), None),
        check_vma=False,
    )
```

```python
import jax
import jax.numpy as jnp
from jax import lax
from jax.experimental import pallas as pl
from jax.experimental.pallas import tpu as pltpu
from jax.sharding import PartitionSpec as P

HEADS = 12
HEAD = 64
WIDTH = 768
HALF = WIDTH // 2
HIDDEN = 3072
ROWS = 512
BLOCK = 128
BLOCKS = 4
DP = 8
PEERS = 128
EPS = 1e-06
NEGATIVE = -1e30
GROUPS = ((0, 32), (32, 32), (64, 32), (96, 32))
CHUNK = 32
ORDER = (4, 2, 6, 1, 3, 5, 7)
MESH = pl.DeviceIdType.MESH
F32 = jnp.float32
BF16 = jnp.bfloat16


def matmul(left, right):
    return jnp.dot(left, right, preferred_element_type=F32)


def matmul_nt(left, right):
    return lax.dot_general(
        left, right, (((1,), (1,)), ((), ())), preferred_element_type=F32
    )


def layer_norm(values):
    centred = values - jnp.mean(values, axis=-1, keepdims=True)
    variance = jnp.mean(centred * centred, axis=-1, keepdims=True)
    return centred * lax.rsqrt(variance + EPS)


def gelu(values):
    return 0.5 * values * (1.0 + lax.erf(values * 0.7071067811865476))


def iota(shape, dim):
    return lax.broadcasted_iota(jnp.int32, shape, dim)


def one_hot(condition):
    return jnp.where(condition, 1.0, 0.0).astype(BF16)


def kernel(
    patches_hbm, owner_ref, segment_ref, mask_ref, in_hbm, out_hbm, keys_hbm, up_hbm, down_hbm,
    result_ref,
    patches, w_in, w_out, w_keys, w_up, w_down,
    stage, slots, place_out, place_in,
    seg_col, image_col, bias, arrived_joint, context, hidden, moe_normed,
    slot_send, slot_recv, back_send, back_recv, rows_in, rows_out, mix_weights,
    load_sem, block_send_sem, block_recv_sem, place_send_sem, place_recv_sem,
    slot_send_sem, slot_recv_sem, back_send_sem, back_recv_sem, plane_sem, cube_sem,
):
    dp, ex = lax.axis_index("dp"), lax.axis_index("expert")
    y, core = lax.div(dp, 2), lax.rem(dp, 2)
    z, x = lax.div(ex, 4), lax.rem(ex, 4)

    dp_at = [[lax.rem(y + ay, 4) * 2 + lax.rem(core + ac, 2) for ac in range(2)] for ay in range(4)]
    ex_at = [[lax.rem(z + az, 4) * 4 + lax.rem(x + ax, 4) for ax in range(4)] for az in range(4)]

    def peer(k, sign):
        ax = k % 4
        ay, az, ac = (k // 16 + ax) % 4, (k // 4 + ax) % 4, k // 64
        return (dp_at[sign * ay % 4][ac], ex_at[sign * az % 4][sign * ax % 4])

    barrier = pltpu.get_barrier_semaphore()
    line_dp = [(dp_at[a % 4][a // 4], ex) for a in range(1, DP)]
    line_z = [(dp, ex_at[a][0]) for a in range(1, 4)]
    line_x = [(dp, ex_at[0][a]) for a in range(1, 4)]

    def tell(semaphore, line):
        for device in line:
            pl.semaphore_signal(semaphore, inc=1, device_id=device, device_id_type=MESH)

    tell(barrier, line_dp + line_z + line_x)

    loads = [
        pltpu.make_async_copy(source, target, load_sem.at[i])
        for i, (source, target) in enumerate(
            (
                (patches_hbm, patches),
                (in_hbm, w_in),
                (keys_hbm, w_keys),
                (out_hbm, w_out),
                (up_hbm.at[0], w_up),
                (down_hbm.at[0], w_down),
            )
        )
    ]
    for load in loads:
        load.start()

    targets = [lax.div(owner_ref[b], BLOCKS * PEERS // DP) for b in range(BLOCKS)]
    places = [lax.rem(owner_ref[b], BLOCKS) for b in range(BLOCKS)]

    loads[0].wait()
    for a in range(DP):
        to = dp_at[a % 4][a // 4]
        index, place = jnp.int32(0), jnp.int32(-1)
        for b in range(BLOCKS):
            hit = targets[b] == to
            index = jnp.where(hit, b, index)
            place = jnp.where(hit, places[b], place)
        if a:
            stage[a] = patches[index]
            place_out[a] = jnp.full((8, 128), place, jnp.int32)
        else:
            slots[0] = patches[index]
            place_in[0] = jnp.full((8, 128), place, jnp.int32)

    pl.semaphore_wait(barrier, 13)
    sends = {}
    for a in ORDER:
        to = (dp_at[a % 4][a // 4], ex)
        for source, target, send, recv in (
            (place_out, place_in, place_send_sem, place_recv_sem),
            (stage, slots, block_send_sem, block_recv_sem),
        ):
            copy = pltpu.make_async_remote_copy(
                src_ref=source.at[a], dst_ref=target.at[a], send_sem=send.at[a], recv_sem=recv.at[a],
                device_id=to, device_id_type=MESH,
            )
            copy.start()
            sends.setdefault(a, []).append(copy)

    tell(plane_sem, line_x)
    segment = segment_ref[...]
    seg_col[...] = jnp.transpose(jnp.broadcast_to(segment.astype(F32), (BLOCK, ROWS)))
    image_col[...] = jnp.transpose(
        jnp.broadcast_to((segment & (BLOCKS - 1)).astype(F32), (BLOCK, ROWS))
    )
    for a in range(BLOCKS):
        for b in range(BLOCKS):
            link = jnp.where(mask_ref[a, b] == 1, 0.0, NEGATIVE)
            rows, columns = slice(a * BLOCK, (a + 1) * BLOCK), slice(b * BLOCK, (b + 1) * BLOCK)
            same = seg_col[rows, :] == segment[:, columns].astype(F32)
            bias[rows, columns] = jnp.where(same, link, NEGATIVE)

    pl.semaphore_wait(plane_sem, 3)
    tell(cube_sem, line_dp)
    k_lane = iota((PEERS, PEERS), 1)
    ax = k_lane & 3
    az = ((k_lane >> 2) + ax) & 3
    ay = ((k_lane >> 4) + ax) & 3
    ac = k_lane >> 6
    expert_at = ((((y + ay) & 3) * 2 + ((core + ac) & 1)) * 4 + ((z + az) & 3)) * 4 + ((x + ax) & 3)
    reorder = one_hot(iota((PEERS, PEERS), 0) == expert_at)
    for load in loads[1:3]:
        load.wait()
    keys = matmul(w_keys[...], reorder).astype(BF16)

    def arrive(a):
        rows = layer_norm(slots[a].astype(F32)).astype(BF16)
        for c in range(3):
            columns = slice(c * WIDTH, (c + 1) * WIDTH)
            arrived_joint[a, :, columns] = matmul(rows, w_in[:, columns]).astype(BF16)

    arrive(0)
    for a in ORDER:
        for copy in sends[a]:
            copy.wait()
        arrive(a)
    pl.semaphore_wait(cube_sem, DP - 1)
    source = []
    for p in range(BLOCKS):
        where_from = jnp.zeros((8, 128), jnp.int32)
        for a in range(1, DP):
            where_from = jnp.where(place_in[a] == p, a, where_from)
        source.append(jnp.max(where_from))

    lane = iota((BLOCK, BLOCK), 1)
    first = lane < HEAD
    scales = [jnp.where(first == (h == 0), HEAD**-0.5, 0.0).astype(BF16) for h in range(2)]

    ones = jnp.ones((ROWS, BLOCK), BF16)
    for i in range(HEADS // 2):
        columns = slice(i * BLOCK, (i + 1) * BLOCK)

        def placed(part):
            at = slice(part * WIDTH + i * BLOCK, part * WIDTH + (i + 1) * BLOCK)
            return [arrived_joint[index, :, at] for index in source]

        query_blocks = placed(0)
        key_rows = jnp.concatenate(placed(1), axis=0)
        both = jnp.concatenate([jnp.concatenate(placed(2), axis=0), ones], axis=1)
        for q in range(BLOCKS):
            rows = slice(q * BLOCK, (q + 1) * BLOCK)
            queries = query_blocks[q]
            stacked = jnp.concatenate([queries * scale for scale in scales], axis=0)
            scores = matmul_nt(stacked, key_rows)
            raised = []
            for h in range(2):
                linked = scores[h * BLOCK : (h + 1) * BLOCK, :] + bias[rows, :]
                raised.append(jnp.exp(linked - jnp.max(linked, axis=1, keepdims=True)).astype(BF16))
            sums = matmul(jnp.concatenate(raised, axis=0), both)
            parts = sums[:, :BLOCK] / sums[:, BLOCK:]
            context[rows, columns] = jnp.where(first, parts[:BLOCK], parts[BLOCK:]).astype(BF16)

    loads[3].wait()
    ordered = jnp.concatenate([slots[index] for index in source], axis=0)
    added = ordered.astype(F32) + matmul(context[...], w_out[...])
    hidden[...] = added.astype(BF16)
    moe_normed[...] = layer_norm(hidden[...].astype(F32)).astype(BF16)
    logits = matmul(moe_normed[...], keys)

    image = image_col[...]
    members = [image == float(s) for s in range(BLOCKS)]

    def by_image(per_image):
        chosen = per_image[0]
        for s in range(1, BLOCKS):
            chosen = jnp.where(members[s], per_image[s], chosen)
        return chosen

    column_max = [
        jnp.max(jnp.where(m, logits, NEGATIVE), axis=0, keepdims=True) for m in members
    ]
    raised = jnp.exp(logits - by_image(column_max))
    totals = [jnp.sum(jnp.where(m, raised, 0.0), axis=0, keepdims=True) for m in members]
    dispatch = jnp.transpose(raised / by_image(totals)).astype(BF16)

    halves = jnp.concatenate([moe_normed[:, :HALF], moe_normed[:, HALF:]], axis=0)
    image_row = segment & (BLOCKS - 1)
    eight = CHUNK * 8
    row = iota((eight, ROWS), 0)
    spread = one_hot(lax.broadcasted_iota(jnp.int32, (eight, CHUNK), 0) >> 3 == iota((eight, CHUNK), 1))
    own_image = ((row >> 1) & 3) == image_row

    def send(k, source, target, send_sem, recv_sem, sign):
        recv = recv_sem.at[sum(k >= first + count for first, count in GROUPS)]
        if k:
            pltpu.make_async_remote_copy(
                src_ref=source.at[k], dst_ref=target.at[k], send_sem=send_sem, recv_sem=recv,
                device_id=peer(k, sign), device_id_type=MESH,
            ).start()
        else:
            pltpu.make_async_copy(source.at[0], target.at[0], recv).start()

    for c in range(PEERS // CHUNK):
        wide = matmul(spread, dispatch[c * CHUNK : (c + 1) * CHUNK, :])
        weights = [
            jnp.where(own_image & ((row & 1) == h), wide, 0.0).astype(BF16) for h in range(2)
        ]
        summed = matmul(jnp.concatenate(weights, axis=1), halves)
        slot_send[c * CHUNK : (c + 1) * CHUNK] = summed.reshape(CHUNK, 8, HALF).astype(BF16)
        for k in range(c * CHUNK, (c + 1) * CHUNK):
            send(k, slot_send, slot_recv, slot_send_sem, slot_recv_sem, 1)

    top = jnp.exp(logits - jnp.max(logits, axis=1, keepdims=True))
    combine = (top / jnp.sum(top, axis=1, keepdims=True)).astype(BF16)
    column = iota((BLOCK, PEERS * 8), 1)
    repeat = one_hot(iota((PEERS, PEERS * 8), 1) >> 3 == iota((PEERS, PEERS * 8), 0))
    for q in range(BLOCKS):
        rows = slice(q * BLOCK, (q + 1) * BLOCK)
        wide = matmul(combine[rows, :], repeat)
        for c in range(PEERS * 8 // BLOCK):
            columns = slice(c * BLOCK, (c + 1) * BLOCK)
            slot = column[:, columns]
            own = ((slot >> 1) & 3).astype(F32) == image[rows, :]
            for h in range(2):
                mix_weights[h, rows, columns] = jnp.where(
                    own & ((slot & 1) == h), wide[:, columns], 0.0
                ).astype(BF16)

    for load in loads[4:]:
        load.wait()
    four = CHUNK * 4
    pick = [one_hot(iota((four, eight), 1) == 2 * iota((four, eight), 0) + h) for h in range(2)]
    weave_q = iota((eight, eight), 1)
    weave = one_hot(
        iota((eight, eight), 0) == 2 * (weave_q & (four - 1)) + lax.shift_right_logical(weave_q, 7)
    )
    for g, (begin, count) in enumerate(GROUPS):
        group = slot_recv.at[pl.ds(begin, count)]
        pltpu.make_async_copy(group, group, slot_recv_sem.at[g]).wait()
        for c in range(count // CHUNK):
            start = begin + c * CHUNK
            arrived = slot_recv[start : start + CHUNK].reshape(eight, HALF)
            for h in range(2):
                rows_in[c * four : (c + 1) * four, h * HALF : (h + 1) * HALF] = matmul(
                    pick[h], arrived
                ).astype(BF16)
        left = rows_in[: count * 4, :]
        total = jnp.zeros((count * 4, WIDTH), F32)
        step = 512
        for c in range(HIDDEN // step):
            inner = gelu(matmul(left, w_up[:, c * step : (c + 1) * step])).astype(BF16)
            total = total + matmul(inner, w_down[c * step : (c + 1) * step, :])
        rows_out[: count * 4, :] = total.astype(BF16)
        for c in range(count // CHUNK):
            start = begin + c * CHUNK
            rows = slice(c * four, (c + 1) * four)
            stacked = jnp.concatenate([rows_out[rows, :HALF], rows_out[rows, HALF:]], axis=0)
            back_send[start : start + CHUNK] = (
                matmul(weave, stacked).reshape(CHUNK, 8, HALF).astype(BF16)
            )
        for k in range(begin, begin + count):
            send(k, back_send, back_recv, back_send_sem, back_recv_sem, -1)

    mixture = [jnp.zeros((ROWS, HALF), F32)] * 2
    for g, (begin, count) in enumerate(GROUPS):
        group = back_recv.at[pl.ds(begin, count)]
        pltpu.make_async_copy(group, group, back_recv_sem.at[g]).wait()
        arrived = back_recv[begin : begin + count].reshape(count * 8, HALF)
        columns = slice(begin * 8, (begin + count) * 8)
        mixture = [mixture[h] + matmul(mix_weights[h, :, columns], arrived) for h in range(2)]
    for h in range(2):
        columns = slice(h * HALF, (h + 1) * HALF)
        result_ref[:, columns] = (hidden[:, columns].astype(F32) + mixture[h]).astype(BF16)

    sent = slot_send.at[pl.ds(1, PEERS - 1)]
    pltpu.make_async_copy(sent, sent, slot_send_sem).wait()
    sent = back_send.at[pl.ds(1, PEERS - 1)]
    pltpu.make_async_copy(sent, sent, back_send_sem).wait()


def per_device(
    patches, owner_slot, segment_ids, block_mask, project_in, project_out, slot_keys, expert_in, expert_out
):
    hbm, smem = pl.BlockSpec(memory_space=pl.ANY), pl.BlockSpec(memory_space=pltpu.SMEM)
    vmem = pl.BlockSpec(memory_space=pltpu.VMEM)
    exchange = pltpu.VMEM((PEERS, 8, HALF), BF16)
    dma = pltpu.SemaphoreType.DMA
    return pl.pallas_call(
        kernel,
        out_shape=jax.ShapeDtypeStruct((ROWS, WIDTH), BF16),
        in_specs=[hbm, smem, vmem, smem, hbm, hbm, hbm, hbm, hbm],
        out_specs=vmem,
        scratch_shapes=[
            pltpu.VMEM((BLOCKS, BLOCK, WIDTH), BF16),
            pltpu.VMEM((WIDTH, 3 * WIDTH), BF16),
            pltpu.VMEM((WIDTH, WIDTH), BF16),
            pltpu.VMEM((WIDTH, PEERS), BF16),
            pltpu.VMEM((WIDTH, HIDDEN), BF16),
            pltpu.VMEM((HIDDEN, WIDTH), BF16),
            pltpu.VMEM((DP, BLOCK, WIDTH), BF16),
            pltpu.VMEM((DP, BLOCK, WIDTH), BF16),
            pltpu.VMEM((DP, 8, 128), jnp.int32),
            pltpu.VMEM((DP, 8, 128), jnp.int32),
            pltpu.VMEM((ROWS, BLOCK), F32),
            pltpu.VMEM((ROWS, BLOCK), F32),
            pltpu.VMEM((ROWS, ROWS), F32),
            pltpu.VMEM((DP, BLOCK, 3 * WIDTH), BF16),
            pltpu.VMEM((ROWS, WIDTH), BF16),
            pltpu.VMEM((ROWS, WIDTH), BF16),
            pltpu.VMEM((ROWS, WIDTH), BF16),
            exchange,
            exchange,
            exchange,
            exchange,
            pltpu.VMEM((max(n for _, n in GROUPS) * 4, WIDTH), BF16),
            pltpu.VMEM((max(n for _, n in GROUPS) * 4, WIDTH), BF16),
            pltpu.VMEM((2, ROWS, PEERS * 8), BF16),
            dma((6,)),
            dma((DP,)),
            dma((DP,)),
            dma((DP,)),
            dma((DP,)),
            dma,
            dma((len(GROUPS),)),
            dma,
            dma((len(GROUPS),)),
            pltpu.SemaphoreType.REGULAR,
            pltpu.SemaphoreType.REGULAR,
        ],
        compiler_params=pltpu.CompilerParams(
            collective_id=0, has_side_effects=True, vmem_limit_bytes=58 * 1024 * 1024
        ),
    )(
        patches.reshape(BLOCKS, BLOCK, WIDTH),
        owner_slot,
        segment_ids.reshape(1, ROWS),
        block_mask,
        project_in,
        project_out,
        slot_keys,
        expert_in,
        expert_out,
    )


def solution(mesh):
    in_specs = (
        P(("dp", "expert"), None),
        P(("dp", "expert")),
        P(("dp", "expert")),
        P(("dp", "expert"), None),
        P(),
        P(),
        P(),
        P(("dp", "expert"), None, None),
        P(("dp", "expert"), None, None),
    )
    return jax.shard_map(
        per_device,
        mesh=mesh,
        in_specs=in_specs,
        out_specs=P(("dp", "expert"), None),
        check_vma=False,
    )
```

```python
import jax
import jax.numpy as jnp
from jax import lax
from jax.experimental import pallas as pl
from jax.experimental.pallas import tpu as pltpu
from jax.sharding import PartitionSpec as P

HEADS = 12
HEAD = 64
WIDTH = 768
HALF = WIDTH // 2
HIDDEN = 3072
ROWS = 512
BLOCK = 128
BLOCKS = 4
DP = 8
PEERS = 128
EPS = 1e-06
NEGATIVE = -1e30
GROUPS = ((0, 32), (32, 32), (64, 32), (96, 32))
CHUNK = 32
ORDER = (4, 2, 6, 1, 3, 5, 7)
MESH = pl.DeviceIdType.MESH
F32 = jnp.float32
BF16 = jnp.bfloat16


def matmul(left, right):
    return jnp.dot(left, right, preferred_element_type=F32)


def matmul_nt(left, right):
    return lax.dot_general(
        left, right, (((1,), (1,)), ((), ())), preferred_element_type=F32
    )


def layer_norm(values):
    centred = values - jnp.mean(values, axis=-1, keepdims=True)
    variance = jnp.mean(centred * centred, axis=-1, keepdims=True)
    return centred * lax.rsqrt(variance + EPS)


def gelu(values):
    return 0.5 * values * (1.0 + lax.erf(values * 0.7071067811865476))


def iota(shape, dim):
    return lax.broadcasted_iota(jnp.int32, shape, dim)


def one_hot(condition):
    return jnp.where(condition, 1.0, 0.0).astype(BF16)


def kernel(
    patches_hbm, owner_ref, segment_ref, mask_ref, in_hbm, out_hbm, keys_hbm, up_hbm, down_hbm,
    result_ref,
    patches, w_in, w_out, w_keys, w_up, w_down,
    stage, slots, place_out, place_in,
    seg_col, image_col, bias, arrived_joint, context, hidden, moe_normed,
    slot_send, slot_recv, back_send, back_recv, rows_in, rows_out, mix_weights,
    load_sem, block_send_sem, block_recv_sem, place_send_sem, place_recv_sem,
    slot_send_sem, slot_recv_sem, back_send_sem, back_recv_sem, plane_sem, cube_sem,
):
    dp, ex = lax.axis_index("dp"), lax.axis_index("expert")
    y, core = lax.div(dp, 2), lax.rem(dp, 2)
    z, x = lax.div(ex, 4), lax.rem(ex, 4)

    dp_at = [[lax.rem(y + ay, 4) * 2 + lax.rem(core + ac, 2) for ac in range(2)] for ay in range(4)]
    ex_at = [[lax.rem(z + az, 4) * 4 + lax.rem(x + ax, 4) for ax in range(4)] for az in range(4)]

    def peer(k, sign):
        ax = k % 4
        ay, az, ac = (k // 16 + ax) % 4, (k // 4 + ax) % 4, k // 64
        return (dp_at[sign * ay % 4][ac], ex_at[sign * az % 4][sign * ax % 4])

    barrier = pltpu.get_barrier_semaphore()
    line_dp = [(dp_at[a % 4][a // 4], ex) for a in range(1, DP)]
    line_z = [(dp, ex_at[a][0]) for a in range(1, 4)]
    line_x = [(dp, ex_at[0][a]) for a in range(1, 4)]

    def tell(semaphore, line):
        for device in line:
            pl.semaphore_signal(semaphore, inc=1, device_id=device, device_id_type=MESH)

    tell(barrier, line_dp + line_z + line_x)

    loads = [
        pltpu.make_async_copy(source, target, load_sem.at[i])
        for i, (source, target) in enumerate(
            (
                (patches_hbm, patches),
                (in_hbm, w_in),
                (keys_hbm, w_keys),
                (out_hbm, w_out),
                (up_hbm.at[0], w_up),
                (down_hbm.at[0], w_down),
            )
        )
    ]
    for load in loads:
        load.start()

    targets = [lax.div(owner_ref[b], BLOCKS * PEERS // DP) for b in range(BLOCKS)]
    places = [lax.rem(owner_ref[b], BLOCKS) for b in range(BLOCKS)]

    loads[0].wait()
    for a in range(DP):
        to = dp_at[a % 4][a // 4]
        index, place = jnp.int32(0), jnp.int32(-1)
        for b in range(BLOCKS):
            hit = targets[b] == to
            index = jnp.where(hit, b, index)
            place = jnp.where(hit, places[b], place)
        if a:
            stage[a] = patches[index]
            place_out[a] = jnp.full((8, 128), place, jnp.int32)
        else:
            slots[0] = patches[index]
            place_in[0] = jnp.full((8, 128), place, jnp.int32)

    pl.semaphore_wait(barrier, 13)
    sends = {}
    for a in ORDER:
        to = (dp_at[a % 4][a // 4], ex)
        for source, target, send, recv in (
            (place_out, place_in, place_send_sem, place_recv_sem),
            (stage, slots, block_send_sem, block_recv_sem),
        ):
            copy = pltpu.make_async_remote_copy(
                src_ref=source.at[a], dst_ref=target.at[a], send_sem=send.at[a], recv_sem=recv.at[a],
                device_id=to, device_id_type=MESH,
            )
            copy.start()
            sends.setdefault(a, []).append(copy)

    tell(plane_sem, line_x)
    segment = segment_ref[...]
    seg_col[...] = jnp.transpose(jnp.broadcast_to(segment.astype(F32), (BLOCK, ROWS)))
    image_col[...] = jnp.transpose(
        jnp.broadcast_to((segment & (BLOCKS - 1)).astype(F32), (BLOCK, ROWS))
    )
    for a in range(BLOCKS):
        for b in range(BLOCKS):
            link = jnp.where(mask_ref[a, b] == 1, 0.0, NEGATIVE)
            rows, columns = slice(a * BLOCK, (a + 1) * BLOCK), slice(b * BLOCK, (b + 1) * BLOCK)
            same = seg_col[rows, :] == segment[:, columns].astype(F32)
            bias[rows, columns] = jnp.where(same, link, NEGATIVE)

    pl.semaphore_wait(plane_sem, 3)
    tell(cube_sem, line_dp)
    k_lane = iota((PEERS, PEERS), 1)
    ax = k_lane & 3
    az = ((k_lane >> 2) + ax) & 3
    ay = ((k_lane >> 4) + ax) & 3
    ac = k_lane >> 6
    expert_at = ((((y + ay) & 3) * 2 + ((core + ac) & 1)) * 4 + ((z + az) & 3)) * 4 + ((x + ax) & 3)
    reorder = one_hot(iota((PEERS, PEERS), 0) == expert_at)
    for load in loads[1:3]:
        load.wait()
    keys = matmul(w_keys[...], reorder).astype(BF16)

    def arrive(a):
        rows = layer_norm(slots[a].astype(F32)).astype(BF16)
        for c in range(3):
            columns = slice(c * WIDTH, (c + 1) * WIDTH)
            arrived_joint[a, :, columns] = matmul(rows, w_in[:, columns]).astype(BF16)

    arrive(0)
    for a in ORDER:
        for copy in sends[a]:
            copy.wait()
        arrive(a)
    pl.semaphore_wait(cube_sem, DP - 1)
    source = []
    for p in range(BLOCKS):
        where_from = jnp.zeros((8, 128), jnp.int32)
        for a in range(1, DP):
            where_from = jnp.where(place_in[a] == p, a, where_from)
        source.append(jnp.max(where_from))

    lane = iota((BLOCK, BLOCK), 1)
    first = lane < HEAD
    scales = [jnp.where(first == (h == 0), HEAD**-0.5, 0.0).astype(BF16) for h in range(2)]

    ones = jnp.ones((ROWS, BLOCK), BF16)
    for i in range(HEADS // 2):
        columns = slice(i * BLOCK, (i + 1) * BLOCK)

        def placed(part):
            at = slice(part * WIDTH + i * BLOCK, part * WIDTH + (i + 1) * BLOCK)
            return [arrived_joint[index, :, at] for index in source]

        query_blocks = placed(0)
        key_rows = jnp.concatenate(placed(1), axis=0)
        both = jnp.concatenate([jnp.concatenate(placed(2), axis=0), ones], axis=1)
        for q in range(BLOCKS):
            rows = slice(q * BLOCK, (q + 1) * BLOCK)
            queries = query_blocks[q]
            stacked = jnp.concatenate([queries * scale for scale in scales], axis=0)
            scores = matmul_nt(stacked, key_rows)
            raised = []
            for h in range(2):
                linked = scores[h * BLOCK : (h + 1) * BLOCK, :] + bias[rows, :]
                raised.append(jnp.exp(linked - jnp.max(linked, axis=1, keepdims=True)).astype(BF16))
            sums = matmul(jnp.concatenate(raised, axis=0), both)
            parts = sums[:, :BLOCK] / sums[:, BLOCK:]
            context[rows, columns] = jnp.where(first, parts[:BLOCK], parts[BLOCK:]).astype(BF16)

    loads[3].wait()
    ordered = jnp.concatenate([slots[index] for index in source], axis=0)
    added = ordered.astype(F32) + matmul(context[...], w_out[...])
    hidden[...] = added.astype(BF16)
    moe_normed[...] = layer_norm(hidden[...].astype(F32)).astype(BF16)
    logits = matmul(moe_normed[...], keys)

    image = image_col[...]
    members = [image == float(s) for s in range(BLOCKS)]

    def by_image(per_image):
        chosen = per_image[0]
        for s in range(1, BLOCKS):
            chosen = jnp.where(members[s], per_image[s], chosen)
        return chosen

    column_max = [
        jnp.max(jnp.where(m, logits, NEGATIVE), axis=0, keepdims=True) for m in members
    ]
    raised = jnp.exp(logits - by_image(column_max))
    totals = [jnp.sum(jnp.where(m, raised, 0.0), axis=0, keepdims=True) for m in members]
    dispatch = jnp.transpose(raised / by_image(totals)).astype(BF16)

    halves = jnp.concatenate([moe_normed[:, :HALF], moe_normed[:, HALF:]], axis=0)
    image_row = segment & (BLOCKS - 1)
    eight = CHUNK * 8
    row = iota((eight, ROWS), 0)
    spread = one_hot(lax.broadcasted_iota(jnp.int32, (eight, CHUNK), 0) >> 3 == iota((eight, CHUNK), 1))
    own_image = ((row >> 1) & 3) == image_row

    def send(k, source, target, send_sem, recv_sem, sign):
        recv = recv_sem.at[sum(k >= first + count for first, count in GROUPS)]
        if k:
            pltpu.make_async_remote_copy(
                src_ref=source.at[k], dst_ref=target.at[k], send_sem=send_sem, recv_sem=recv,
                device_id=peer(k, sign), device_id_type=MESH,
            ).start()
        else:
            pltpu.make_async_copy(source.at[0], target.at[0], recv).start()

    for c in range(PEERS // CHUNK):
        wide = matmul(spread, dispatch[c * CHUNK : (c + 1) * CHUNK, :])
        weights = [
            jnp.where(own_image & ((row & 1) == h), wide, 0.0).astype(BF16) for h in range(2)
        ]
        summed = matmul(jnp.concatenate(weights, axis=1), halves)
        slot_send[c * CHUNK : (c + 1) * CHUNK] = summed.reshape(CHUNK, 8, HALF).astype(BF16)
        for k in range(c * CHUNK, (c + 1) * CHUNK):
            send(k, slot_send, slot_recv, slot_send_sem, slot_recv_sem, 1)

    for load in loads[4:]:
        load.wait()
    four = CHUNK * 4
    pick = [one_hot(iota((four, eight), 1) == 2 * iota((four, eight), 0) + h) for h in range(2)]
    weave_q = iota((eight, eight), 1)
    weave = one_hot(
        iota((eight, eight), 0) == 2 * (weave_q & (four - 1)) + lax.shift_right_logical(weave_q, 7)
    )
    for g, (begin, count) in enumerate(GROUPS):
        group = slot_recv.at[pl.ds(begin, count)]
        pltpu.make_async_copy(group, group, slot_recv_sem.at[g]).wait()
        for c in range(count // CHUNK):
            start = begin + c * CHUNK
            arrived = slot_recv[start : start + CHUNK].reshape(eight, HALF)
            for h in range(2):
                rows_in[c * four : (c + 1) * four, h * HALF : (h + 1) * HALF] = matmul(
                    pick[h], arrived
                ).astype(BF16)
        left = rows_in[: count * 4, :]
        total = jnp.zeros((count * 4, WIDTH), F32)
        step = 1536
        for c in range(HIDDEN // step):
            inner = gelu(matmul(left, w_up[:, c * step : (c + 1) * step])).astype(BF16)
            total = total + matmul(inner, w_down[c * step : (c + 1) * step, :])
        rows_out[: count * 4, :] = total.astype(BF16)
        for c in range(count // CHUNK):
            start = begin + c * CHUNK
            rows = slice(c * four, (c + 1) * four)
            stacked = jnp.concatenate([rows_out[rows, :HALF], rows_out[rows, HALF:]], axis=0)
            back_send[start : start + CHUNK] = (
                matmul(weave, stacked).reshape(CHUNK, 8, HALF).astype(BF16)
            )
        for k in range(begin, begin + count):
            send(k, back_send, back_recv, back_send_sem, back_recv_sem, -1)

    top = jnp.exp(logits - jnp.max(logits, axis=1, keepdims=True))
    combine = (top / jnp.sum(top, axis=1, keepdims=True)).astype(BF16)
    column = iota((BLOCK, PEERS * 8), 1)
    repeat = one_hot(iota((PEERS, PEERS * 8), 1) >> 3 == iota((PEERS, PEERS * 8), 0))
    for q in range(BLOCKS):
        rows = slice(q * BLOCK, (q + 1) * BLOCK)
        wide = matmul(combine[rows, :], repeat)
        for c in range(PEERS * 8 // BLOCK):
            columns = slice(c * BLOCK, (c + 1) * BLOCK)
            slot = column[:, columns]
            own = ((slot >> 1) & 3).astype(F32) == image[rows, :]
            for h in range(2):
                mix_weights[h, rows, columns] = jnp.where(
                    own & ((slot & 1) == h), wide[:, columns], 0.0
                ).astype(BF16)

    mixture = [jnp.zeros((ROWS, HALF), F32)] * 2
    for g, (begin, count) in enumerate(GROUPS):
        group = back_recv.at[pl.ds(begin, count)]
        pltpu.make_async_copy(group, group, back_recv_sem.at[g]).wait()
        arrived = back_recv[begin : begin + count].reshape(count * 8, HALF)
        columns = slice(begin * 8, (begin + count) * 8)
        mixture = [mixture[h] + matmul(mix_weights[h, :, columns], arrived) for h in range(2)]
    for h in range(2):
        columns = slice(h * HALF, (h + 1) * HALF)
        result_ref[:, columns] = (hidden[:, columns].astype(F32) + mixture[h]).astype(BF16)

    sent = slot_send.at[pl.ds(1, PEERS - 1)]
    pltpu.make_async_copy(sent, sent, slot_send_sem).wait()
    sent = back_send.at[pl.ds(1, PEERS - 1)]
    pltpu.make_async_copy(sent, sent, back_send_sem).wait()


def per_device(
    patches, owner_slot, segment_ids, block_mask, project_in, project_out, slot_keys, expert_in, expert_out
):
    hbm, smem = pl.BlockSpec(memory_space=pl.ANY), pl.BlockSpec(memory_space=pltpu.SMEM)
    vmem = pl.BlockSpec(memory_space=pltpu.VMEM)
    exchange = pltpu.VMEM((PEERS, 8, HALF), BF16)
    dma = pltpu.SemaphoreType.DMA
    return pl.pallas_call(
        kernel,
        out_shape=jax.ShapeDtypeStruct((ROWS, WIDTH), BF16),
        in_specs=[hbm, smem, vmem, smem, hbm, hbm, hbm, hbm, hbm],
        out_specs=vmem,
        scratch_shapes=[
            pltpu.VMEM((BLOCKS, BLOCK, WIDTH), BF16),
            pltpu.VMEM((WIDTH, 3 * WIDTH), BF16),
            pltpu.VMEM((WIDTH, WIDTH), BF16),
            pltpu.VMEM((WIDTH, PEERS), BF16),
            pltpu.VMEM((WIDTH, HIDDEN), BF16),
            pltpu.VMEM((HIDDEN, WIDTH), BF16),
            pltpu.VMEM((DP, BLOCK, WIDTH), BF16),
            pltpu.VMEM((DP, BLOCK, WIDTH), BF16),
            pltpu.VMEM((DP, 8, 128), jnp.int32),
            pltpu.VMEM((DP, 8, 128), jnp.int32),
            pltpu.VMEM((ROWS, BLOCK), F32),
            pltpu.VMEM((ROWS, BLOCK), F32),
            pltpu.VMEM((ROWS, ROWS), F32),
            pltpu.VMEM((DP, BLOCK, 3 * WIDTH), BF16),
            pltpu.VMEM((ROWS, WIDTH), BF16),
            pltpu.VMEM((ROWS, WIDTH), BF16),
            pltpu.VMEM((ROWS, WIDTH), BF16),
            exchange,
            exchange,
            exchange,
            exchange,
            pltpu.VMEM((max(n for _, n in GROUPS) * 4, WIDTH), BF16),
            pltpu.VMEM((max(n for _, n in GROUPS) * 4, WIDTH), BF16),
            pltpu.VMEM((2, ROWS, PEERS * 8), BF16),
            dma((6,)),
            dma((DP,)),
            dma((DP,)),
            dma((DP,)),
            dma((DP,)),
            dma,
            dma((len(GROUPS),)),
            dma,
            dma((len(GROUPS),)),
            pltpu.SemaphoreType.REGULAR,
            pltpu.SemaphoreType.REGULAR,
        ],
        compiler_params=pltpu.CompilerParams(
            collective_id=0, has_side_effects=True, vmem_limit_bytes=58 * 1024 * 1024
        ),
    )(
        patches.reshape(BLOCKS, BLOCK, WIDTH),
        owner_slot,
        segment_ids.reshape(1, ROWS),
        block_mask,
        project_in,
        project_out,
        slot_keys,
        expert_in,
        expert_out,
    )


def solution(mesh):
    in_specs = (
        P(("dp", "expert"), None),
        P(("dp", "expert")),
        P(("dp", "expert")),
        P(("dp", "expert"), None),
        P(),
        P(),
        P(),
        P(("dp", "expert"), None, None),
        P(("dp", "expert"), None, None),
    )
    return jax.shard_map(
        per_device,
        mesh=mesh,
        in_specs=in_specs,
        out_specs=P(("dp", "expert"), None),
        check_vma=False,
    )
```

```python
import jax
import jax.numpy as jnp
from jax import lax
from jax.experimental import pallas as pl
from jax.experimental.pallas import tpu as pltpu
from jax.sharding import PartitionSpec as P

HEADS = 12
HEAD = 64
WIDTH = 768
HALF = WIDTH // 2
HIDDEN = 3072
ROWS = 512
BLOCK = 128
BLOCKS = 4
DP = 8
PEERS = 128
EPS = 1e-06
NEGATIVE = -1e30
GROUPS = ((0, 32), (32, 32), (64, 32), (96, 32))
CHUNK = 32
ORDER = (2, 1, 3, 4, 6, 5, 7)
MESH = pl.DeviceIdType.MESH
F32 = jnp.float32
BF16 = jnp.bfloat16


def matmul(left, right):
    return jnp.dot(left, right, preferred_element_type=F32)


def matmul_nt(left, right):
    return lax.dot_general(
        left, right, (((1,), (1,)), ((), ())), preferred_element_type=F32
    )


def layer_norm(values):
    centred = values - jnp.mean(values, axis=-1, keepdims=True)
    variance = jnp.mean(centred * centred, axis=-1, keepdims=True)
    return centred * lax.rsqrt(variance + EPS)


def gelu(values):
    return 0.5 * values * (1.0 + lax.erf(values * 0.7071067811865476))


def iota(shape, dim):
    return lax.broadcasted_iota(jnp.int32, shape, dim)


def one_hot(condition):
    return jnp.where(condition, 1.0, 0.0).astype(BF16)


def kernel(
    patches_hbm, owner_ref, segment_ref, mask_ref, in_hbm, out_hbm, keys_hbm, up_hbm, down_hbm,
    result_ref,
    patches, w_in, w_out, w_keys, w_up, w_down,
    stage, slots, place_out, place_in,
    seg_col, image_col, bias, arrived_joint, context, hidden, moe_normed,
    slot_send, slot_recv, back_send, back_recv, rows_in, rows_out, mix_weights,
    load_sem, block_send_sem, block_recv_sem, place_send_sem, place_recv_sem,
    slot_send_sem, slot_recv_sem, back_send_sem, back_recv_sem, plane_sem, cube_sem,
):
    dp, ex = lax.axis_index("dp"), lax.axis_index("expert")
    y, core = lax.div(dp, 2), lax.rem(dp, 2)
    z, x = lax.div(ex, 4), lax.rem(ex, 4)

    dp_at = [[lax.rem(y + ay, 4) * 2 + lax.rem(core + ac, 2) for ac in range(2)] for ay in range(4)]
    ex_at = [[lax.rem(z + az, 4) * 4 + lax.rem(x + ax, 4) for ax in range(4)] for az in range(4)]

    def peer(k, sign):
        ax = k % 4
        ay, az, ac = (k // 16 + ax) % 4, (k // 4 + ax) % 4, k // 64
        return (dp_at[sign * ay % 4][ac], ex_at[sign * az % 4][sign * ax % 4])

    barrier = pltpu.get_barrier_semaphore()
    line_dp = [(dp_at[a % 4][a // 4], ex) for a in range(1, DP)]
    line_z = [(dp, ex_at[a][0]) for a in range(1, 4)]
    line_x = [(dp, ex_at[0][a]) for a in range(1, 4)]

    def tell(semaphore, line):
        for device in line:
            pl.semaphore_signal(semaphore, inc=1, device_id=device, device_id_type=MESH)

    tell(barrier, line_dp + line_z + line_x)

    loads = [
        pltpu.make_async_copy(source, target, load_sem.at[i])
        for i, (source, target) in enumerate(
            (
                (patches_hbm, patches),
                (in_hbm, w_in),
                (keys_hbm, w_keys),
                (out_hbm, w_out),
                (up_hbm.at[0], w_up),
                (down_hbm.at[0], w_down),
            )
        )
    ]
    for load in loads:
        load.start()

    targets = [lax.div(owner_ref[b], BLOCKS * PEERS // DP) for b in range(BLOCKS)]
    places = [lax.rem(owner_ref[b], BLOCKS) for b in range(BLOCKS)]

    loads[0].wait()
    for a in range(DP):
        to = dp_at[a % 4][a // 4]
        index, place = jnp.int32(0), jnp.int32(-1)
        for b in range(BLOCKS):
            hit = targets[b] == to
            index = jnp.where(hit, b, index)
            place = jnp.where(hit, places[b], place)
        if a:
            stage[a] = patches[index]
            place_out[a] = jnp.full((8, 128), place, jnp.int32)
        else:
            slots[0] = patches[index]
            place_in[0] = jnp.full((8, 128), place, jnp.int32)

    pl.semaphore_wait(barrier, 13)
    sends = {}
    for a in ORDER:
        to = (dp_at[a % 4][a // 4], ex)
        for source, target, send, recv in (
            (place_out, place_in, place_send_sem, place_recv_sem),
            (stage, slots, block_send_sem, block_recv_sem),
        ):
            copy = pltpu.make_async_remote_copy(
                src_ref=source.at[a], dst_ref=target.at[a], send_sem=send.at[a], recv_sem=recv.at[a],
                device_id=to, device_id_type=MESH,
            )
            copy.start()
            sends.setdefault(a, []).append(copy)

    tell(plane_sem, line_x)
    segment = segment_ref[...]
    seg_col[...] = jnp.transpose(jnp.broadcast_to(segment.astype(F32), (BLOCK, ROWS)))
    image_col[...] = jnp.transpose(
        jnp.broadcast_to((segment & (BLOCKS - 1)).astype(F32), (BLOCK, ROWS))
    )
    for a in range(BLOCKS):
        for b in range(BLOCKS):
            link = jnp.where(mask_ref[a, b] == 1, 0.0, NEGATIVE)
            rows, columns = slice(a * BLOCK, (a + 1) * BLOCK), slice(b * BLOCK, (b + 1) * BLOCK)
            same = seg_col[rows, :] == segment[:, columns].astype(F32)
            bias[rows, columns] = jnp.where(same, link, NEGATIVE)

    pl.semaphore_wait(plane_sem, 3)
    tell(cube_sem, line_dp)
    k_lane = iota((PEERS, PEERS), 1)
    ax = k_lane & 3
    az = ((k_lane >> 2) + ax) & 3
    ay = ((k_lane >> 4) + ax) & 3
    ac = k_lane >> 6
    expert_at = ((((y + ay) & 3) * 2 + ((core + ac) & 1)) * 4 + ((z + az) & 3)) * 4 + ((x + ax) & 3)
    reorder = one_hot(iota((PEERS, PEERS), 0) == expert_at)
    for load in loads[1:3]:
        load.wait()
    keys = matmul(w_keys[...], reorder).astype(BF16)

    def arrive(a):
        rows = layer_norm(slots[a].astype(F32)).astype(BF16)
        for c in range(3):
            columns = slice(c * WIDTH, (c + 1) * WIDTH)
            arrived_joint[a, :, columns] = matmul(rows, w_in[:, columns]).astype(BF16)

    arrive(0)
    for a in ORDER:
        for copy in sends[a]:
            copy.wait()
        arrive(a)
    pl.semaphore_wait(cube_sem, DP - 1)
    source = []
    for p in range(BLOCKS):
        where_from = jnp.zeros((8, 128), jnp.int32)
        for a in range(1, DP):
            where_from = jnp.where(place_in[a] == p, a, where_from)
        source.append(jnp.max(where_from))

    lane = iota((BLOCK, BLOCK), 1)
    first = lane < HEAD
    scales = [jnp.where(first == (h == 0), HEAD**-0.5, 0.0).astype(BF16) for h in range(2)]

    ones = jnp.ones((ROWS, BLOCK), BF16)
    for i in range(HEADS // 2):
        columns = slice(i * BLOCK, (i + 1) * BLOCK)

        def placed(part):
            at = slice(part * WIDTH + i * BLOCK, part * WIDTH + (i + 1) * BLOCK)
            return [arrived_joint[index, :, at] for index in source]

        query_blocks = placed(0)
        key_rows = jnp.concatenate(placed(1), axis=0)
        both = jnp.concatenate([jnp.concatenate(placed(2), axis=0), ones], axis=1)
        for q in range(BLOCKS):
            rows = slice(q * BLOCK, (q + 1) * BLOCK)
            queries = query_blocks[q]
            stacked = jnp.concatenate([queries * scale for scale in scales], axis=0)
            scores = matmul_nt(stacked, key_rows)
            raised = []
            for h in range(2):
                linked = scores[h * BLOCK : (h + 1) * BLOCK, :] + bias[rows, :]
                raised.append(jnp.exp(linked - jnp.max(linked, axis=1, keepdims=True)).astype(BF16))
            sums = matmul(jnp.concatenate(raised, axis=0), both)
            parts = sums[:, :BLOCK] / sums[:, BLOCK:]
            context[rows, columns] = jnp.where(first, parts[:BLOCK], parts[BLOCK:]).astype(BF16)

    loads[3].wait()
    ordered = jnp.concatenate([slots[index] for index in source], axis=0)
    added = ordered.astype(F32) + matmul(context[...], w_out[...])
    hidden[...] = added.astype(BF16)
    moe_normed[...] = layer_norm(hidden[...].astype(F32)).astype(BF16)
    logits = matmul(moe_normed[...], keys)

    image = image_col[...]
    members = [image == float(s) for s in range(BLOCKS)]

    def by_image(per_image):
        chosen = per_image[0]
        for s in range(1, BLOCKS):
            chosen = jnp.where(members[s], per_image[s], chosen)
        return chosen

    column_max = [
        jnp.max(jnp.where(m, logits, NEGATIVE), axis=0, keepdims=True) for m in members
    ]
    raised = jnp.exp(logits - by_image(column_max))
    totals = [jnp.sum(jnp.where(m, raised, 0.0), axis=0, keepdims=True) for m in members]
    dispatch = jnp.transpose(raised / by_image(totals)).astype(BF16)

    halves = jnp.concatenate([moe_normed[:, :HALF], moe_normed[:, HALF:]], axis=0)
    image_row = segment & (BLOCKS - 1)
    eight = CHUNK * 8
    row = iota((eight, ROWS), 0)
    spread = one_hot(lax.broadcasted_iota(jnp.int32, (eight, CHUNK), 0) >> 3 == iota((eight, CHUNK), 1))
    own_image = ((row >> 1) & 3) == image_row

    def send(k, source, target, send_sem, recv_sem, sign):
        recv = recv_sem.at[sum(k >= first + count for first, count in GROUPS)]
        if k:
            pltpu.make_async_remote_copy(
                src_ref=source.at[k], dst_ref=target.at[k], send_sem=send_sem, recv_sem=recv,
                device_id=peer(k, sign), device_id_type=MESH,
            ).start()
        else:
            pltpu.make_async_copy(source.at[0], target.at[0], recv).start()

    for c in range(PEERS // CHUNK):
        wide = matmul(spread, dispatch[c * CHUNK : (c + 1) * CHUNK, :])
        weights = [
            jnp.where(own_image & ((row & 1) == h), wide, 0.0).astype(BF16) for h in range(2)
        ]
        summed = matmul(jnp.concatenate(weights, axis=1), halves)
        slot_send[c * CHUNK : (c + 1) * CHUNK] = summed.reshape(CHUNK, 8, HALF).astype(BF16)
        for k in range(c * CHUNK, (c + 1) * CHUNK):
            send(k, slot_send, slot_recv, slot_send_sem, slot_recv_sem, 1)

    for load in loads[4:]:
        load.wait()
    four = CHUNK * 4
    pick = [one_hot(iota((four, eight), 1) == 2 * iota((four, eight), 0) + h) for h in range(2)]
    weave_q = iota((eight, eight), 1)
    weave = one_hot(
        iota((eight, eight), 0) == 2 * (weave_q & (four - 1)) + lax.shift_right_logical(weave_q, 7)
    )
    for g, (begin, count) in enumerate(GROUPS):
        group = slot_recv.at[pl.ds(begin, count)]
        pltpu.make_async_copy(group, group, slot_recv_sem.at[g]).wait()
        for c in range(count // CHUNK):
            start = begin + c * CHUNK
            arrived = slot_recv[start : start + CHUNK].reshape(eight, HALF)
            for h in range(2):
                rows_in[c * four : (c + 1) * four, h * HALF : (h + 1) * HALF] = matmul(
                    pick[h], arrived
                ).astype(BF16)
        left = rows_in[: count * 4, :]
        total = jnp.zeros((count * 4, WIDTH), F32)
        step = 1536
        for c in range(HIDDEN // step):
            inner = gelu(matmul(left, w_up[:, c * step : (c + 1) * step])).astype(BF16)
            total = total + matmul(inner, w_down[c * step : (c + 1) * step, :])
        rows_out[: count * 4, :] = total.astype(BF16)
        for c in range(count // CHUNK):
            start = begin + c * CHUNK
            rows = slice(c * four, (c + 1) * four)
            stacked = jnp.concatenate([rows_out[rows, :HALF], rows_out[rows, HALF:]], axis=0)
            back_send[start : start + CHUNK] = (
                matmul(weave, stacked).reshape(CHUNK, 8, HALF).astype(BF16)
            )
        for k in range(begin, begin + count):
            send(k, back_send, back_recv, back_send_sem, back_recv_sem, -1)

    top = jnp.exp(logits - jnp.max(logits, axis=1, keepdims=True))
    combine = (top / jnp.sum(top, axis=1, keepdims=True)).astype(BF16)
    column = iota((BLOCK, PEERS * 8), 1)
    repeat = one_hot(iota((PEERS, PEERS * 8), 1) >> 3 == iota((PEERS, PEERS * 8), 0))
    for q in range(BLOCKS):
        rows = slice(q * BLOCK, (q + 1) * BLOCK)
        wide = matmul(combine[rows, :], repeat)
        for c in range(PEERS * 8 // BLOCK):
            columns = slice(c * BLOCK, (c + 1) * BLOCK)
            slot = column[:, columns]
            own = ((slot >> 1) & 3).astype(F32) == image[rows, :]
            for h in range(2):
                mix_weights[h, rows, columns] = jnp.where(
                    own & ((slot & 1) == h), wide[:, columns], 0.0
                ).astype(BF16)

    mixture = [jnp.zeros((ROWS, HALF), F32)] * 2
    for g, (begin, count) in enumerate(GROUPS):
        group = back_recv.at[pl.ds(begin, count)]
        pltpu.make_async_copy(group, group, back_recv_sem.at[g]).wait()
        arrived = back_recv[begin : begin + count].reshape(count * 8, HALF)
        columns = slice(begin * 8, (begin + count) * 8)
        mixture = [mixture[h] + matmul(mix_weights[h, :, columns], arrived) for h in range(2)]
    for h in range(2):
        columns = slice(h * HALF, (h + 1) * HALF)
        result_ref[:, columns] = (hidden[:, columns].astype(F32) + mixture[h]).astype(BF16)

    sent = slot_send.at[pl.ds(1, PEERS - 1)]
    pltpu.make_async_copy(sent, sent, slot_send_sem).wait()
    sent = back_send.at[pl.ds(1, PEERS - 1)]
    pltpu.make_async_copy(sent, sent, back_send_sem).wait()


def per_device(
    patches, owner_slot, segment_ids, block_mask, project_in, project_out, slot_keys, expert_in, expert_out
):
    hbm, smem = pl.BlockSpec(memory_space=pl.ANY), pl.BlockSpec(memory_space=pltpu.SMEM)
    vmem = pl.BlockSpec(memory_space=pltpu.VMEM)
    exchange = pltpu.VMEM((PEERS, 8, HALF), BF16)
    dma = pltpu.SemaphoreType.DMA
    return pl.pallas_call(
        kernel,
        out_shape=jax.ShapeDtypeStruct((ROWS, WIDTH), BF16),
        in_specs=[hbm, smem, vmem, smem, hbm, hbm, hbm, hbm, hbm],
        out_specs=vmem,
        scratch_shapes=[
            pltpu.VMEM((BLOCKS, BLOCK, WIDTH), BF16),
            pltpu.VMEM((WIDTH, 3 * WIDTH), BF16),
            pltpu.VMEM((WIDTH, WIDTH), BF16),
            pltpu.VMEM((WIDTH, PEERS), BF16),
            pltpu.VMEM((WIDTH, HIDDEN), BF16),
            pltpu.VMEM((HIDDEN, WIDTH), BF16),
            pltpu.VMEM((DP, BLOCK, WIDTH), BF16),
            pltpu.VMEM((DP, BLOCK, WIDTH), BF16),
            pltpu.VMEM((DP, 8, 128), jnp.int32),
            pltpu.VMEM((DP, 8, 128), jnp.int32),
            pltpu.VMEM((ROWS, BLOCK), F32),
            pltpu.VMEM((ROWS, BLOCK), F32),
            pltpu.VMEM((ROWS, ROWS), F32),
            pltpu.VMEM((DP, BLOCK, 3 * WIDTH), BF16),
            pltpu.VMEM((ROWS, WIDTH), BF16),
            pltpu.VMEM((ROWS, WIDTH), BF16),
            pltpu.VMEM((ROWS, WIDTH), BF16),
            exchange,
            exchange,
            exchange,
            exchange,
            pltpu.VMEM((max(n for _, n in GROUPS) * 4, WIDTH), BF16),
            pltpu.VMEM((max(n for _, n in GROUPS) * 4, WIDTH), BF16),
            pltpu.VMEM((2, ROWS, PEERS * 8), BF16),
            dma((6,)),
            dma((DP,)),
            dma((DP,)),
            dma((DP,)),
            dma((DP,)),
            dma,
            dma((len(GROUPS),)),
            dma,
            dma((len(GROUPS),)),
            pltpu.SemaphoreType.REGULAR,
            pltpu.SemaphoreType.REGULAR,
        ],
        compiler_params=pltpu.CompilerParams(
            collective_id=0, has_side_effects=True, vmem_limit_bytes=58 * 1024 * 1024
        ),
    )(
        patches.reshape(BLOCKS, BLOCK, WIDTH),
        owner_slot,
        segment_ids.reshape(1, ROWS),
        block_mask,
        project_in,
        project_out,
        slot_keys,
        expert_in,
        expert_out,
    )


def solution(mesh):
    in_specs = (
        P(("dp", "expert"), None),
        P(("dp", "expert")),
        P(("dp", "expert")),
        P(("dp", "expert"), None),
        P(),
        P(),
        P(),
        P(("dp", "expert"), None, None),
        P(("dp", "expert"), None, None),
    )
    return jax.shard_map(
        per_device,
        mesh=mesh,
        in_specs=in_specs,
        out_specs=P(("dp", "expert"), None),
        check_vma=False,
    )
```

```python
import jax
import jax.numpy as jnp
from jax import lax
from jax.experimental import pallas as pl
from jax.experimental.pallas import tpu as pltpu
from jax.sharding import PartitionSpec as P

HEADS = 12
HEAD = 64
WIDTH = 768
HALF = WIDTH // 2
HIDDEN = 3072
ROWS = 512
BLOCK = 128
BLOCKS = 4
DP = 8
PEERS = 128
EPS = 1e-06
NEGATIVE = -1e30
GROUPS = ((0, 32), (32, 32), (64, 32), (96, 32))
CHUNK = 32
ORDER = (4, 2, 6, 1, 3, 5, 7)
MESH = pl.DeviceIdType.MESH
F32 = jnp.float32
BF16 = jnp.bfloat16


def matmul(left, right):
    return jnp.dot(left, right, preferred_element_type=F32)


def matmul_nt(left, right):
    return lax.dot_general(
        left, right, (((1,), (1,)), ((), ())), preferred_element_type=F32
    )


def layer_norm(values):
    centred = values - jnp.mean(values, axis=-1, keepdims=True)
    variance = jnp.mean(centred * centred, axis=-1, keepdims=True)
    return centred * lax.rsqrt(variance + EPS)


def gelu(values):
    return 0.5 * values * (1.0 + lax.erf(values * 0.7071067811865476))


def iota(shape, dim):
    return lax.broadcasted_iota(jnp.int32, shape, dim)


def one_hot(condition):
    return jnp.where(condition, 1.0, 0.0).astype(BF16)


def kernel(
    patches_hbm, owner_ref, segment_ref, mask_ref, in_hbm, out_hbm, keys_hbm, up_hbm, down_hbm,
    result_ref,
    patches, w_in, w_out, w_keys, w_up, w_down,
    stage, slots, place_out, place_in,
    seg_col, image_col, bias, arrived_joint, context, hidden, moe_normed,
    slot_send, slot_recv, back_send, back_recv, rows_in, rows_out, mix_weights,
    load_sem, block_send_sem, block_recv_sem, place_send_sem, place_recv_sem,
    slot_send_sem, slot_recv_sem, back_send_sem, back_recv_sem, plane_sem, cube_sem,
):
    dp, ex = lax.axis_index("dp"), lax.axis_index("expert")
    y, core = lax.div(dp, 2), lax.rem(dp, 2)
    z, x = lax.div(ex, 4), lax.rem(ex, 4)

    dp_at = [[lax.rem(y + ay, 4) * 2 + lax.rem(core + ac, 2) for ac in range(2)] for ay in range(4)]
    ex_at = [[lax.rem(z + az, 4) * 4 + lax.rem(x + ax, 4) for ax in range(4)] for az in range(4)]

    def peer(k, sign):
        ax = k % 4
        ay, az, ac = (k // 16 + ax) % 4, (k // 4 + ax) % 4, k // 64
        return (dp_at[sign * ay % 4][ac], ex_at[sign * az % 4][sign * ax % 4])

    barrier = pltpu.get_barrier_semaphore()
    line_dp = [(dp_at[a % 4][a // 4], ex) for a in range(1, DP)]
    line_z = [(dp, ex_at[a][0]) for a in range(1, 4)]
    line_x = [(dp, ex_at[0][a]) for a in range(1, 4)]

    def tell(semaphore, line):
        for device in line:
            pl.semaphore_signal(semaphore, inc=1, device_id=device, device_id_type=MESH)

    tell(barrier, line_dp + line_z + line_x)

    loads = [
        pltpu.make_async_copy(source, target, load_sem.at[i])
        for i, (source, target) in enumerate(
            (
                (patches_hbm, patches),
                (in_hbm, w_in),
                (keys_hbm, w_keys),
                (out_hbm, w_out),
                (up_hbm.at[0], w_up),
                (down_hbm.at[0], w_down),
            )
        )
    ]
    for load in loads:
        load.start()

    targets = [lax.div(owner_ref[b], BLOCKS * PEERS // DP) for b in range(BLOCKS)]
    places = [lax.rem(owner_ref[b], BLOCKS) for b in range(BLOCKS)]

    loads[0].wait()
    for a in range(DP):
        to = dp_at[a % 4][a // 4]
        index, place = jnp.int32(0), jnp.int32(-1)
        for b in range(BLOCKS):
            hit = targets[b] == to
            index = jnp.where(hit, b, index)
            place = jnp.where(hit, places[b], place)
        if a:
            stage[a] = patches[index]
            place_out[a] = jnp.full((8, 128), place, jnp.int32)
        else:
            slots[0] = patches[index]
            place_in[0] = jnp.full((8, 128), place, jnp.int32)

    pl.semaphore_wait(barrier, 13)
    sends = {}
    for a in ORDER:
        to = (dp_at[a % 4][a // 4], ex)
        for source, target, send, recv in (
            (place_out, place_in, place_send_sem, place_recv_sem),
            (stage, slots, block_send_sem, block_recv_sem),
        ):
            copy = pltpu.make_async_remote_copy(
                src_ref=source.at[a], dst_ref=target.at[a], send_sem=send.at[a], recv_sem=recv.at[a],
                device_id=to, device_id_type=MESH,
            )
            copy.start()
            sends.setdefault(a, []).append(copy)

    tell(plane_sem, line_x)
    segment = segment_ref[...]
    seg_col[...] = jnp.transpose(jnp.broadcast_to(segment.astype(F32), (BLOCK, ROWS)))
    image_col[...] = jnp.transpose(
        jnp.broadcast_to((segment & (BLOCKS - 1)).astype(F32), (BLOCK, ROWS))
    )
    for a in range(BLOCKS):
        for b in range(BLOCKS):
            link = jnp.where(mask_ref[a, b] == 1, 0.0, NEGATIVE)
            rows, columns = slice(a * BLOCK, (a + 1) * BLOCK), slice(b * BLOCK, (b + 1) * BLOCK)
            same = seg_col[rows, :] == segment[:, columns].astype(F32)
            bias[rows, columns] = jnp.where(same, link, NEGATIVE)

    pl.semaphore_wait(plane_sem, 3)
    tell(cube_sem, line_dp)
    k_lane = iota((PEERS, PEERS), 1)
    ax = k_lane & 3
    az = ((k_lane >> 2) + ax) & 3
    ay = ((k_lane >> 4) + ax) & 3
    ac = k_lane >> 6
    expert_at = ((((y + ay) & 3) * 2 + ((core + ac) & 1)) * 4 + ((z + az) & 3)) * 4 + ((x + ax) & 3)
    reorder = one_hot(iota((PEERS, PEERS), 0) == expert_at)
    for load in loads[1:3]:
        load.wait()
    keys = matmul(w_keys[...], reorder).astype(BF16)

    def arrive(a):
        rows = layer_norm(slots[a].astype(F32)).astype(BF16)
        for c in range(3):
            columns = slice(c * WIDTH, (c + 1) * WIDTH)
            arrived_joint[a, :, columns] = matmul(rows, w_in[:, columns]).astype(BF16)

    arrive(0)
    for a in ORDER:
        for copy in sends[a]:
            copy.wait()
        arrive(a)
    pl.semaphore_wait(cube_sem, DP - 1)
    source = []
    for p in range(BLOCKS):
        where_from = jnp.zeros((8, 128), jnp.int32)
        for a in range(1, DP):
            where_from = jnp.where(place_in[a] == p, a, where_from)
        source.append(jnp.max(where_from))

    lane = iota((2 * BLOCK, BLOCK), 1)
    first = lane < HEAD
    scales = [jnp.where(first == (h == 0), HEAD**-0.5, 0.0).astype(BF16) for h in range(2)]

    ones = jnp.ones((ROWS, BLOCK), BF16)
    for i in range(HEADS // 2):
        columns = slice(i * BLOCK, (i + 1) * BLOCK)

        def placed(part):
            at = slice(part * WIDTH + i * BLOCK, part * WIDTH + (i + 1) * BLOCK)
            return [arrived_joint[index, :, at] for index in source]

        query_blocks = placed(0)
        key_rows = jnp.concatenate(placed(1), axis=0)
        both = jnp.concatenate([jnp.concatenate(placed(2), axis=0), ones], axis=1)
        for q in (0, 2):
            rows, pair = slice(q * BLOCK, (q + 2) * BLOCK), 2 * BLOCK
            queries = jnp.concatenate(query_blocks[q : q + 2], axis=0)
            stacked = jnp.concatenate([queries * scale for scale in scales], axis=0)
            scores = matmul_nt(stacked, key_rows)
            raised = []
            for h in range(2):
                linked = scores[h * pair : (h + 1) * pair, :] + bias[rows, :]
                raised.append(jnp.exp(linked - jnp.max(linked, axis=1, keepdims=True)).astype(BF16))
            sums = matmul(jnp.concatenate(raised, axis=0), both)
            parts = sums[:, :BLOCK] / sums[:, BLOCK:]
            context[rows, columns] = jnp.where(first, parts[:pair], parts[pair:]).astype(BF16)

    loads[3].wait()
    ordered = jnp.concatenate([slots[index] for index in source], axis=0)
    added = ordered.astype(F32) + matmul(context[...], w_out[...])
    hidden[...] = added.astype(BF16)
    moe_normed[...] = layer_norm(hidden[...].astype(F32)).astype(BF16)
    logits = matmul(moe_normed[...], keys)

    image = image_col[...]
    members = [image == float(s) for s in range(BLOCKS)]

    def by_image(per_image):
        chosen = per_image[0]
        for s in range(1, BLOCKS):
            chosen = jnp.where(members[s], per_image[s], chosen)
        return chosen

    column_max = [
        jnp.max(jnp.where(m, logits, NEGATIVE), axis=0, keepdims=True) for m in members
    ]
    raised = jnp.exp(logits - by_image(column_max))
    totals = [jnp.sum(jnp.where(m, raised, 0.0), axis=0, keepdims=True) for m in members]
    dispatch = jnp.transpose(raised / by_image(totals)).astype(BF16)

    halves = jnp.concatenate([moe_normed[:, :HALF], moe_normed[:, HALF:]], axis=0)
    image_row = segment & (BLOCKS - 1)
    eight = CHUNK * 8
    row = iota((eight, ROWS), 0)
    spread = one_hot(lax.broadcasted_iota(jnp.int32, (eight, CHUNK), 0) >> 3 == iota((eight, CHUNK), 1))
    own_image = ((row >> 1) & 3) == image_row

    def send(k, source, target, send_sem, recv_sem, sign):
        recv = recv_sem.at[sum(k >= first + count for first, count in GROUPS)]
        if k:
            pltpu.make_async_remote_copy(
                src_ref=source.at[k], dst_ref=target.at[k], send_sem=send_sem, recv_sem=recv,
                device_id=peer(k, sign), device_id_type=MESH,
            ).start()
        else:
            pltpu.make_async_copy(source.at[0], target.at[0], recv).start()

    for c in range(PEERS // CHUNK):
        wide = matmul(spread, dispatch[c * CHUNK : (c + 1) * CHUNK, :])
        weights = [
            jnp.where(own_image & ((row & 1) == h), wide, 0.0).astype(BF16) for h in range(2)
        ]
        summed = matmul(jnp.concatenate(weights, axis=1), halves)
        slot_send[c * CHUNK : (c + 1) * CHUNK] = summed.reshape(CHUNK, 8, HALF).astype(BF16)
        for k in range(c * CHUNK, (c + 1) * CHUNK):
            send(k, slot_send, slot_recv, slot_send_sem, slot_recv_sem, 1)

    for load in loads[4:]:
        load.wait()
    four = CHUNK * 4
    pick = [one_hot(iota((four, eight), 1) == 2 * iota((four, eight), 0) + h) for h in range(2)]
    weave_q = iota((eight, eight), 1)
    weave = one_hot(
        iota((eight, eight), 0) == 2 * (weave_q & (four - 1)) + lax.shift_right_logical(weave_q, 7)
    )
    for g, (begin, count) in enumerate(GROUPS):
        group = slot_recv.at[pl.ds(begin, count)]
        pltpu.make_async_copy(group, group, slot_recv_sem.at[g]).wait()
        for c in range(count // CHUNK):
            start = begin + c * CHUNK
            arrived = slot_recv[start : start + CHUNK].reshape(eight, HALF)
            for h in range(2):
                rows_in[c * four : (c + 1) * four, h * HALF : (h + 1) * HALF] = matmul(
                    pick[h], arrived
                ).astype(BF16)
        left = rows_in[: count * 4, :]
        total = jnp.zeros((count * 4, WIDTH), F32)
        step = 1536
        for c in range(HIDDEN // step):
            inner = gelu(matmul(left, w_up[:, c * step : (c + 1) * step])).astype(BF16)
            total = total + matmul(inner, w_down[c * step : (c + 1) * step, :])
        rows_out[: count * 4, :] = total.astype(BF16)
        for c in range(count // CHUNK):
            start = begin + c * CHUNK
            rows = slice(c * four, (c + 1) * four)
            stacked = jnp.concatenate([rows_out[rows, :HALF], rows_out[rows, HALF:]], axis=0)
            back_send[start : start + CHUNK] = (
                matmul(weave, stacked).reshape(CHUNK, 8, HALF).astype(BF16)
            )
        for k in range(begin, begin + count):
            send(k, back_send, back_recv, back_send_sem, back_recv_sem, -1)

    top = jnp.exp(logits - jnp.max(logits, axis=1, keepdims=True))
    combine = (top / jnp.sum(top, axis=1, keepdims=True)).astype(BF16)
    column = iota((BLOCK, PEERS * 8), 1)
    repeat = one_hot(iota((PEERS, PEERS * 8), 1) >> 3 == iota((PEERS, PEERS * 8), 0))
    for q in range(BLOCKS):
        rows = slice(q * BLOCK, (q + 1) * BLOCK)
        wide = matmul(combine[rows, :], repeat)
        for c in range(PEERS * 8 // BLOCK):
            columns = slice(c * BLOCK, (c + 1) * BLOCK)
            slot = column[:, columns]
            own = ((slot >> 1) & 3).astype(F32) == image[rows, :]
            for h in range(2):
                mix_weights[h, rows, columns] = jnp.where(
                    own & ((slot & 1) == h), wide[:, columns], 0.0
                ).astype(BF16)

    mixture = [jnp.zeros((ROWS, HALF), F32)] * 2
    for g, (begin, count) in enumerate(GROUPS):
        group = back_recv.at[pl.ds(begin, count)]
        pltpu.make_async_copy(group, group, back_recv_sem.at[g]).wait()
        arrived = back_recv[begin : begin + count].reshape(count * 8, HALF)
        columns = slice(begin * 8, (begin + count) * 8)
        mixture = [mixture[h] + matmul(mix_weights[h, :, columns], arrived) for h in range(2)]
    for h in range(2):
        columns = slice(h * HALF, (h + 1) * HALF)
        result_ref[:, columns] = (hidden[:, columns].astype(F32) + mixture[h]).astype(BF16)

    sent = slot_send.at[pl.ds(1, PEERS - 1)]
    pltpu.make_async_copy(sent, sent, slot_send_sem).wait()
    sent = back_send.at[pl.ds(1, PEERS - 1)]
    pltpu.make_async_copy(sent, sent, back_send_sem).wait()


def per_device(
    patches, owner_slot, segment_ids, block_mask, project_in, project_out, slot_keys, expert_in, expert_out
):
    hbm, smem = pl.BlockSpec(memory_space=pl.ANY), pl.BlockSpec(memory_space=pltpu.SMEM)
    vmem = pl.BlockSpec(memory_space=pltpu.VMEM)
    exchange = pltpu.VMEM((PEERS, 8, HALF), BF16)
    dma = pltpu.SemaphoreType.DMA
    return pl.pallas_call(
        kernel,
        out_shape=jax.ShapeDtypeStruct((ROWS, WIDTH), BF16),
        in_specs=[hbm, smem, vmem, smem, hbm, hbm, hbm, hbm, hbm],
        out_specs=vmem,
        scratch_shapes=[
            pltpu.VMEM((BLOCKS, BLOCK, WIDTH), BF16),
            pltpu.VMEM((WIDTH, 3 * WIDTH), BF16),
            pltpu.VMEM((WIDTH, WIDTH), BF16),
            pltpu.VMEM((WIDTH, PEERS), BF16),
            pltpu.VMEM((WIDTH, HIDDEN), BF16),
            pltpu.VMEM((HIDDEN, WIDTH), BF16),
            pltpu.VMEM((DP, BLOCK, WIDTH), BF16),
            pltpu.VMEM((DP, BLOCK, WIDTH), BF16),
            pltpu.VMEM((DP, 8, 128), jnp.int32),
            pltpu.VMEM((DP, 8, 128), jnp.int32),
            pltpu.VMEM((ROWS, BLOCK), F32),
            pltpu.VMEM((ROWS, BLOCK), F32),
            pltpu.VMEM((ROWS, ROWS), F32),
            pltpu.VMEM((DP, BLOCK, 3 * WIDTH), BF16),
            pltpu.VMEM((ROWS, WIDTH), BF16),
            pltpu.VMEM((ROWS, WIDTH), BF16),
            pltpu.VMEM((ROWS, WIDTH), BF16),
            exchange,
            exchange,
            exchange,
            exchange,
            pltpu.VMEM((max(n for _, n in GROUPS) * 4, WIDTH), BF16),
            pltpu.VMEM((max(n for _, n in GROUPS) * 4, WIDTH), BF16),
            pltpu.VMEM((2, ROWS, PEERS * 8), BF16),
            dma((6,)),
            dma((DP,)),
            dma((DP,)),
            dma((DP,)),
            dma((DP,)),
            dma,
            dma((len(GROUPS),)),
            dma,
            dma((len(GROUPS),)),
            pltpu.SemaphoreType.REGULAR,
            pltpu.SemaphoreType.REGULAR,
        ],
        compiler_params=pltpu.CompilerParams(
            collective_id=0, has_side_effects=True, vmem_limit_bytes=58 * 1024 * 1024
        ),
    )(
        patches.reshape(BLOCKS, BLOCK, WIDTH),
        owner_slot,
        segment_ids.reshape(1, ROWS),
        block_mask,
        project_in,
        project_out,
        slot_keys,
        expert_in,
        expert_out,
    )


def solution(mesh):
    in_specs = (
        P(("dp", "expert"), None),
        P(("dp", "expert")),
        P(("dp", "expert")),
        P(("dp", "expert"), None),
        P(),
        P(),
        P(),
        P(("dp", "expert"), None, None),
        P(("dp", "expert"), None, None),
    )
    return jax.shard_map(
        per_device,
        mesh=mesh,
        in_specs=in_specs,
        out_specs=P(("dp", "expert"), None),
        check_vma=False,
    )
```
